256 devices in a mesh: lon: 128 (over x, y_lo, z, core), lat: 2 (over y_hi).
Axes of the slice: x: 4, y: 4 (y_hi: 2, y_lo: 2; y = y_hi * 2 + y_lo), z: 8, core: 2. Of those that a mesh axis runs over, the one named last changes fastest.
Arguments:
- counts_blocks: int32 [512, 512, 512], P('lon', 'lat'), may hold values from 0 to 49
- exposure_blocks: float32 [512, 512, 512], P('lon', 'lat'), may hold values from 0.1 to 1
- expo_col: int32 [512], P('lon'), may hold values from 0 to 65535, as said below
- expo_count: int32 [128], P('lon'), may hold values from 1 to 4, as said below
Outputs:
- significance: float32 [3, 512, 65536], P(None, 'lat', 'lon')
The draws below stay inside these ranges and needn't reach their ends.
Inputs may be any that keep to these rules, and one draw needn't show every extreme that they name: `expo_col`: exposure e belongs to lon device i = e // 4; its first sky column is ((i + k) * 512 + o) modulo 65536 with k from -2 to 1 and o from 0 to 511, and its 512 columns run on round the band. Exposures e of lon device i with e modulo 4 below expo_count[i] are observed; the others take no part.
All inputs are finite; a program needn't handle non-finite values.
Results may differ from the reference program's by a relative error of at most 0.00065.
Values sent between devices are 32-bit elements; how exact they have to be, the bound alone decides.
No kernel may reach another device: no remote copies, remote signals or barrier semaphores. Data moves between devices by JAX's collectives and lax.ppermute only.
A program may use at most 128 MiB of HBM per device.

```python
import math
import jax
import jax.numpy as jnp
from jax import lax

EB = 512
TW = 512
RAD = 32
SCALES = 3
REACH = 2
E_CAP = 4
TILES = 128
EXPO = 512


def draw_expo_col(key, part):
    key = jax.random.fold_in(key, 11)
    key_rel, key_off = jax.random.split(key)
    owner = jnp.arange(EXPO, dtype=jnp.int32) // E_CAP
    shift_tiles = jax.random.randint(key_rel, (EXPO,), -REACH, REACH, dtype=jnp.int32)
    within = jax.random.randint(key_off, (EXPO,), 0, TW, dtype=jnp.int32)
    shift_tiles = shift_tiles.at[0].set(-1)
    within = within.at[0].set(TW - 1)
    shift_tiles = shift_tiles.at[1].set(-owner[1])
    within = within.at[1].set(0)
    return ((owner + shift_tiles) * TW + within) % (TW * TILES)


def draw_expo_count(key, part):
    key = jax.random.fold_in(key, 12)
    key_num, key_perm = jax.random.split(key)
    number = jax.random.randint(key_num, (TILES,), 1, E_CAP + 1, dtype=jnp.int32)
    order = jax.random.permutation(key_perm, TILES)
    number = number.at[order[0]].set(E_CAP)
    number = number.at[order[1]].set(1)
    return number


def plant(drawn, key, low, top_value):
    extent = drawn.shape
    spot = [jax.random.randint(jax.random.fold_in(key, axis), (), 0, extent[axis]) for axis in range(len(extent))]
    drawn = drawn.at[tuple(spot)].set(low)
    longest = extent.index(max(extent))
    spot[longest] = (spot[longest] + 1) % extent[longest]
    return drawn.at[tuple(spot)].set(top_value)


def shard_levels(rng, extent, shards, smallest, top_value):
    loudness, own = 1.0, jax.random.fold_in(rng, 6)
    for dim, blocks in shards:
        draws = jnp.exp(jax.random.uniform(jax.random.fold_in(own, dim), (blocks,), jnp.float32, smallest / len(shards), top_value / len(shards)))
        loudness = loudness * jnp.repeat(draws, extent[dim] // blocks).reshape([-1 if axis == dim else 1 for axis in range(len(extent))])
    return loudness


def setup_inputs(seed: int = 0) -> dict:
    key_list = jax.random.split(jax.random.key(seed), 5)
    counts_blocks = plant(jax.random.randint(key_list[0], (EXPO, EB, EB), 0, 50), jax.random.fold_in(key_list[0], 1), 0, 49).astype(jnp.int32)
    exposure_blocks = jnp.clip(jnp.exp(math.log(1.0) - 2.3025851 * jax.random.uniform(key_list[1], (EXPO, EB, EB), jnp.float32) ** shard_levels(key_list[1], (EXPO, EB, EB), ((0, 128), (1, 2)), -0.2, 0.2)), 0.1, 1.0)
    expo_col = draw_expo_col(jax.random.fold_in(key_list[4], 71), 0)
    expo_count = draw_expo_count(jax.random.fold_in(key_list[4], 71), 0)
    return {"counts_blocks": counts_blocks, "exposure_blocks": exposure_blocks, "expo_col": expo_col, "expo_count": expo_count}


def kernel_pair(offset, sigma):
    inside = (jnp.abs(offset) <= RAD).astype(jnp.float32)
    bell = jnp.exp(-offset * offset / (2.0 * sigma * sigma)) * inside
    hat = (1.0 - offset * offset / (sigma * sigma)) * bell
    return (hat, bell)

def column_filter(field, taps):
    width = field.shape[1]
    return jnp.fft.irfft(jnp.fft.rfft(field, axis=1) * jnp.fft.rfft(taps)[None, :], n=width, axis=1)

def reference(counts_blocks, exposure_blocks, expo_col, expo_count):
    height = EB
    width = TW * TILES
    index = jnp.arange(EXPO)
    live = (index % E_CAP < expo_count[index // E_CAP]).astype(jnp.float32)

    def deposit(item, carry):
        sums_c, sums_e = carry
        start = expo_col[item].astype(jnp.int32)
        zero = jnp.zeros((), jnp.int32)
        piece_c = counts_blocks[item].astype(jnp.float32) * live[item]
        piece_e = exposure_blocks[item] * live[item]
        cur_c = lax.dynamic_slice(sums_c, (zero, start), (height, EB))
        cur_e = lax.dynamic_slice(sums_e, (zero, start), (height, EB))
        sums_c = lax.dynamic_update_slice(sums_c, cur_c + piece_c, (zero, start))
        sums_e = lax.dynamic_update_slice(sums_e, cur_e + piece_e, (zero, start))
        return (sums_c, sums_e)
    empty = jnp.zeros((height, width + EB), jnp.float32)
    sums_c, sums_e = lax.fori_loop(0, EXPO, deposit, (empty, empty))
    sky_counts = sums_c[:, :width].at[:, :EB].add(sums_c[:, width:])
    sky_exposure = sums_e[:, :width].at[:, :EB].add(sums_e[:, width:])
    row_rate = lax.optimization_barrier(jnp.sum(sky_counts, axis=1)) / lax.optimization_barrier(jnp.sum(sky_exposure, axis=1))
    background = row_rate[:, None] * sky_exposure
    excess = sky_counts - background
    position = jnp.arange(width)
    col_off = jnp.where(position <= width // 2, position, position - width).astype(jnp.float32)
    row_off = (jnp.arange(height)[None, :] - jnp.arange(height)[:, None]).astype(jnp.float32)
    hp = lax.Precision.HIGHEST
    results = []
    for scale in range(SCALES):
        sigma = RAD / 2.0 ** (4 - scale)
        hat_x, bell_x = kernel_pair(col_off, sigma)
        hat_y, bell_y = kernel_pair(row_off, sigma)
        wavelet = jnp.dot(bell_y, column_filter(excess, hat_x), precision=hp)
        wavelet = wavelet + jnp.dot(hat_y, column_filter(excess, bell_x), precision=hp)
        variance = jnp.dot(bell_y * bell_y, column_filter(background, hat_x * hat_x), precision=hp)
        variance = variance + 2.0 * jnp.dot(hat_y * bell_y, column_filter(background, hat_x * bell_x), precision=hp)
        variance = variance + jnp.dot(hat_y * hat_y, column_filter(background, bell_x * bell_x), precision=hp)
        results.append(wavelet / jnp.sqrt(jnp.maximum(variance, 1.0)))
    return jnp.stack(results)
```

```python
import functools

import jax
import jax.numpy as jnp
import ml_dtypes
import numpy as np
from jax import lax
from jax.experimental import pallas as pl
from jax.experimental.pallas import tpu as pltpu
from jax.sharding import PartitionSpec as P

TW = 512
RAD = 32
SCALES = 3
LON = 128
HALF = 128
FAR_K = 160
NEAR_K = 192
F32 = jnp.float32
BF16 = jnp.bfloat16


def iota(shape, dim):
    return lax.broadcasted_iota(jnp.int32, shape, dim)


def where_am_i():
    lon = lax.axis_index("lon")
    return lon, lax.rem(lon, 2), lax.axis_index("lat")


def pack(x):
    lane = iota((8, 128), 1)
    parts = []
    for j in range(4):
        a = x[32 * j : 32 * j + 8]
        for m in range(1, 4):
            b = pltpu.roll(x[32 * j + 8 * m : 32 * j + 8 * m + 8], 32 * m, 1)
            a = jnp.where(lane < 32 * m, a, b)
        parts.append(a)
    return jnp.concatenate(parts, axis=1)


def unpack(p):
    parts = []
    for j in range(4):
        v = p[:, 128 * j : 128 * j + 128]
        parts.append(v)
        for m in range(1, 4):
            parts.append(pltpu.roll(v, 128 - 32 * m, 1))
    return jnp.concatenate(parts, axis=0)


def slot_place(cols, slot, lon):
    column = cols[slot]
    first = column // TW
    within = column - first * TW
    rel = lax.rem(first - lon + LON + LON // 2, LON) - LON // 2
    return within, rel


def fetch_scalars(cols_hbm, count_hbm, cols, count, sem):
    copies = [
        pltpu.make_async_copy(cols_hbm, cols, sem.at[0]),
        pltpu.make_async_copy(count_hbm, count, sem.at[1]),
    ]
    for copy in copies:
        copy.start()
    return copies


def sums_kernel(count_hbm, c_hbm, e_hbm, sums, acc, count, cbuf, ebuf, ssem, sem):
    scalar = pltpu.make_async_copy(count_hbm, count, ssem)
    scalar.start()
    copies = []
    for slot in range(4):
        copies.append(pltpu.make_async_copy(c_hbm.at[slot], cbuf.at[slot], sem.at[0, slot]))
        copies.append(pltpu.make_async_copy(e_hbm.at[slot], ebuf.at[slot], sem.at[1, slot]))
    for copy in copies:
        copy.start()
    acc[...] = jnp.zeros(acc.shape, F32)
    scalar.wait()
    for slot in range(4):
        copies[2 * slot].wait()
        copies[2 * slot + 1].wait()

        @pl.when(slot < count[0])
        def _(slot=slot):
            def body(g, carry):
                rows = pl.ds(pl.multiple_of(8 * g, 8), 8)
                for f, buf in ((0, cbuf), (1, ebuf)):
                    x = buf[slot, rows, :].astype(F32)
                    x = (x[:, :128] + x[:, 128:256]) + (x[:, 256:384] + x[:, 384:])
                    acc[f, rows, :] += x
                return carry

            lax.fori_loop(0, 2 * HALF // 8, body, 0, unroll=8)

    for f in range(2):
        for j in range(2):
            block = jnp.transpose(acc[f, 128 * j : 128 * j + 128, :])
            sums[f : f + 1, 128 * j : 128 * j + 128] = jnp.sum(block, axis=0, keepdims=True)


def far_kernel(cols_hbm, count_hbm, cbuf, ebuf, near_out, far_out, cols, count, ssem):
    lon, core, lat = where_am_i()
    scalars = fetch_scalars(cols_hbm, count_hbm, cols, count, ssem)
    wanted = jnp.where(core == 1, 1, -2)
    near_out[...] = jnp.zeros(near_out.shape, F32)
    far_out[...] = jnp.zeros(far_out.shape, F32)
    for copy in scalars:
        copy.wait()
    for slot in range(4):
        within, rel = slot_place(cols, slot, lon)

        @pl.when(jnp.logical_and(slot < count[0], rel == wanted))
        def _(slot=slot, within=within):
            lane = iota((8, 128), 1)

            for out, start in ((near_out, HALF * (1 - lat)), (far_out, HALF * lat)):

                def body(g, carry, out=out, start=start):
                    rows = pl.ds(pl.multiple_of(start + 8 * g, 8), 8)
                    here = pl.ds(pl.multiple_of(8 * g, 8), 8)
                    for f, buf in ((0, cbuf), (1, ebuf)):
                        x = rolled(buf, slot, rows, within)
                        for j in range(4):
                            col = lane + 128 * j
                            keep = jnp.where(core == 1, col - within, within - 1 - col) < 0
                            out[f, here, 128 * j : 128 * j + 128] += jnp.where(keep, x[j], 0.0)
                    return carry

                lax.fori_loop(0, HALF // 8, body, 0, unroll=4)


def rolled(buf, slot, rows, within):
    whole = within // 128
    rest = within - 128 * whole
    first = iota((8, 128), 1) < rest
    turned = []
    for j in range(4):
        block = lax.rem(j + 4 - whole, 4)
        x = buf[slot, rows, pl.ds(pl.multiple_of(128 * block, 128), 128)].astype(F32)
        turned.append(pltpu.roll(x, rest, 1))
    return [jnp.where(first, turned[j - 1], turned[j]) for j in range(4)]


def rest_kernel(
    cols_hbm, count_hbm, cbuf, ebuf, q1n, q1f, q0n, q0f, an, af, token, weight, cols, count, ssem
):
    lon, core, lat = where_am_i()
    for copy in fetch_scalars(cols_hbm, count_hbm, cols, count, ssem):
        copy.wait()
    token[...] = jnp.zeros(token.shape, F32)
    sign = 2 * core - 1
    col = iota((8, TW), 1)
    shifts = []
    for slot in range(4):
        within, rel = slot_place(cols, slot, lon)
        alive = slot < count[0]
        shifts.append(within)
        for k, q in enumerate((1, 0, -1, -2)):
            high = jnp.where(jnp.logical_and(alive, rel * sign == q), 1.0, 0.0).astype(F32)
            low = jnp.where(jnp.logical_and(alive, (rel + 1) * sign == q), 1.0, 0.0).astype(F32)
            weight[4 * slot + k] = jnp.where(col >= within, high, low)
    for q1, q0, a, start in ((q1n, q0n, an, HALF * (1 - lat)), (q1f, q0f, af, HALF * lat)):

        def body(g, carry, q1=q1, q0=q0, a=a, start=start):
            rows = pl.ds(pl.multiple_of(start + 8 * g, 8), 8)
            here = pl.ds(pl.multiple_of(8 * g, 8), 8)
            for f, buf in ((0, cbuf), (1, ebuf)):
                xs = [rolled(buf, slot, rows, shifts[slot]) for slot in range(4)]
                for j in range(4):
                    block = slice(128 * j, 128 * j + 128)
                    outs = (q1.at[f], q0.at[f], a.at[0, f], a.at[1, f])
                    for k, out in enumerate(outs):
                        t = xs[0][j] * weight[k, :, block]
                        for slot in range(1, 4):
                            t = t + xs[slot][j] * weight[4 * slot + k, :, block]
                        out[here, block] = t
            return carry

        lax.fori_loop(0, HALF // 8, body, 0, unroll=4)


def merge_kernel(q1, q0, a, b1, partial, message):
    _, core, _ = where_am_i()
    for f in range(2):
        message[f, :HALF, :] = q1[f] + a[1, f]
        mine = q0[f] + a[0, f] + b1[f]
        partial[f] = mine
        edge = jnp.where(core == 1, pltpu.roll(mine[:, 384:], 32, 1), mine[:, :128])
        message[f, HALF:, :] = pack(edge)


def total_kernel(partial, received, sent, total, outer, inner):
    _, core, _ = where_am_i()
    for f in range(2):
        mine = partial[f] + received[f, :HALF, :]
        total[f] = mine
        near = jnp.where(
            core == 1, sent[f, :HALF, :128], pltpu.roll(sent[f, :HALF, 384:], 32, 1)
        )
        outer[f] = unpack(received[f, HALF:, :]) + near
        edge = jnp.where(core == 1, mine[:, :128], pltpu.roll(mine[:, 384:], 32, 1))
        inner[f] = pack(edge)


def seam(total, outer, inner, core):
    lane = iota((HALF, 128), 1)
    left = jnp.where(core == 1, inner, outer)
    right = jnp.where(core == 1, outer, inner)
    a = jnp.where(lane < 96, pltpu.roll(total[:, 384:], 96, 1), pltpu.roll(right, 96, 1))
    b = jnp.where(lane < 32, left, pltpu.roll(total[:, :128], 32, 1))
    return jnp.concatenate([a, b], axis=1)


def seam_kernel(total, outer, inner, wrap, message):
    _, core, lat = where_am_i()
    rows = pl.ds(pl.multiple_of(96 * (1 - lat), 32), 32)
    for f in range(2):
        wrap[f] = seam(total[f], outer[f], unpack(inner[f]), core)
        message[f, :, :TW] = total[f, rows, :]
        message[f, :, TW:] = wrap[f, rows, :]


def bell_hat(offset, sigma):
    inside = jnp.abs(offset) <= RAD
    d = offset.astype(F32)
    bell = jnp.where(inside, jnp.exp(-d * d / (2.0 * sigma * sigma)), 0.0)
    hat = (1.0 - d * d / (sigma * sigma)) * bell
    return bell, hat


def split(x):
    high = x.astype(BF16)
    return high, (x - high.astype(F32)).astype(BF16)


@functools.cache
def tap_scales():
    t = np.arange(-RAD, RAD + 1, dtype=np.float64)
    table = []
    for s in range(SCALES):
        sigma = RAD / 2.0 ** (4 - s)
        g = np.exp(-t * t / (2.0 * sigma * sigma))
        h = (1.0 - t * t / (sigma * sigma)) * g
        row = []
        for k in (h * h, h * g, g * g):
            c = 1.0 + np.arange(4096) / 4096.0
            error = (k * c[:, None]).astype(ml_dtypes.bfloat16).astype(np.float64) / c[:, None] - k
            cost = np.abs(error.sum(1)) / np.abs(k).sum()
            cost = 4.0 * cost + np.sqrt((error**2).sum(1) / (k**2).sum())
            row.append(float(c[np.argmin(cost)]))
        table.append(row)
    return table


def taps_kernel(ctap, cvar, far_tap, near_tap, far_var, near_var, token):
    _, _, lat = where_am_i()
    token[...] = jnp.zeros(token.shape, F32)
    w = iota((256, 128), 0)
    n = iota((256, 128), 1)
    straight = w - n - 64
    wrapped_w = jnp.where(w < 128, 416 + w, w - 160)
    wrapped_n = jnp.where(n < 64, 448 + n, n - 64)
    a = iota((HALF, 128), 0)
    b = iota((HALF, 128), 1)
    table = tap_scales()

    def far_row(p):
        return jnp.where(lat == 0, p, jnp.where(p < HALF, p + HALF, p - 32))

    def near_row(p):
        inner = jnp.where(lat == 0, p + HALF, p)
        adjacent = jnp.where(lat == 0, p - 32, p)
        halo = jnp.where(lat == 0, p + 96, p - 192)
        return jnp.where(p < HALF, inner, jnp.where(p < HALF + 32, adjacent, halo))

    for s in range(SCALES):
        sigma = RAD / 2.0 ** (4 - s)
        chh, chg, cgg = table[s]
        for kind, offset in ((0, straight), (1, wrapped_w - wrapped_n)):
            bell, hat = bell_hat(offset, sigma)
            for k, t in enumerate((hat, bell)):
                high, low = split(t)
                here = slice(256 * s + 128 * k, 256 * s + 128 * k + 128)
                ctap[kind, :256, here] = high
                ctap[kind, 256:512, here] = high
                ctap[kind, 512:, here] = low
            for k, t in enumerate((chh * hat * hat, chg * hat * bell, cgg * bell * bell)):
                here = slice(384 * s + 128 * k, 384 * s + 128 * k + 128)
                t = t.astype(BF16)
                cvar[kind, :256, here] = t
                cvar[kind, 256:, here] = t
        for tap, var, span, place in (
            (far_tap, far_var, FAR_K, far_row),
            (near_tap, near_var, NEAR_K, near_row),
        ):
            for j in range(-(-6 * span // 128)):
                here = slice(128 * j, min(128 * j + 128, 6 * span))
                size = here.stop - here.start
                lane = 128 * j + b
                copy = (lane >= 2 * span).astype(jnp.int32) + (lane >= 4 * span).astype(jnp.int32)
                p = lane - 2 * span * copy
                second = p >= span
                bell, hat = bell_hat(place(jnp.where(second, p - span, p)) - place(a), sigma)
                high, low = split(jnp.where(second, hat, bell))
                t = jnp.where(copy == 1, low.astype(F32), high.astype(F32)).astype(BF16)
                tap[s, :, here] = t[:, :size]
                p = jnp.where(lane >= 3 * span, lane - 3 * span, lane)
                which = (p >= span).astype(jnp.int32) + (p >= 2 * span).astype(jnp.int32)
                bell, hat = bell_hat(place(p - span * which) - place(a), sigma)
                t = jnp.where(which == 1, (2.0 * chg) * hat * bell, chh * hat * hat)
                t = jnp.where(which == 0, cgg * bell * bell, t).astype(BF16)
                var[s, :, here] = t[:, :size]


def mm(a, b):
    return jnp.dot(a, b, preferred_element_type=F32)


def column_filters(size, fields, ctap, cvar, wave, vari, x, xw):
    for j in range(6):
        for f in range(2):
            high, low = split(fields(f, j))
            if j < 4:
                places = [(x, 3 * f + b, j - b) for b in range(3) if j - b in (0, 1)]
            else:
                places = [(xw, f, j - 4)]
            for ref, b, side in places:
                rows = slice(size * b, size * b + size)
                ref[rows, 128 * side : 128 * side + 128] = high
                ref[rows, 256 + 128 * side : 384 + 128 * side] = low
                ref[rows, 512 + 128 * side : 640 + 128 * side] = high
    for f in range(2):
        y = mm(x[3 * size * f : 3 * size * (f + 1), :], ctap[0])
        for s in range(SCALES):
            for k in range(2):
                for b in range(3):
                    wave[s, 2 * f + k, :, 128 * b : 128 * b + 128] = y[
                        size * b : size * b + size, 256 * s + 128 * k : 256 * s + 128 * k + 128
                    ]
    z = mm(x[3 * size :, :512], cvar[0])
    for s in range(SCALES):
        for k in range(3):
            for b in range(3):
                vari[s, k, :, 128 * b : 128 * b + 128] = z[
                    size * b : size * b + size, 384 * s + 128 * k : 384 * s + 128 * k + 128
                ]
    y = mm(xw[...], ctap[1])
    z = mm(xw[size:, :512], cvar[1])
    for s in range(SCALES):
        for k in range(2):
            here = slice(256 * s + 128 * k, 256 * s + 128 * k + 128)
            wave[s, k, :, 384:] = y[:size, here]
            wave[s, 2 + k, :, 384:] = y[size:, here]
        for k in range(3):
            vari[s, k, :, 384:] = z[:, 384 * s + 128 * k : 384 * s + 128 * k + 128]


def near_columns_kernel(total, wrap, ctap, cvar, wave, vari, token, x, xw):
    token[...] = jnp.zeros(token.shape, F32)

    def fields(f, j):
        if j < 4:
            return total[f, :, 128 * j : 128 * j + 128]
        return wrap[f, :, 128 * (j - 4) : 128 * (j - 3)]

    column_filters(HALF, fields, ctap, cvar, wave, vari, x, xw)


def far_columns_kernel(total, outer, inner, lat_rows, ctap, cvar, wave, vari, x, xw):
    _, core, _ = where_am_i()
    wrap = [seam(total[f], outer[f], unpack(inner[f]), core) for f in range(2)]

    def fields(f, j):
        if j < 4:
            mine = total[f, :, 128 * j : 128 * j + 128]
        else:
            mine = wrap[f][:, 128 * (j - 4) : 128 * (j - 3)]
        return jnp.concatenate([mine, lat_rows[f, :, 128 * j : 128 * j + 128]], axis=0)

    column_filters(HALF + RAD, fields, ctap, cvar, wave, vari, x, xw)


def final_kernel(
    near_wave, near_vari, far_wave, far_vari, sums, last,
    far_tap, near_tap, far_var, near_var, out, rate, fw, fv, nw, nv,
):
    _, core, lat = where_am_i()
    whole = sums[...] + last[...]
    own = whole[0:1] / whole[1:2]
    other = whole[2:3] / whole[3:4]
    table = tap_scales()

    def column(row):
        return jnp.transpose(jnp.broadcast_to(row, (128, 128)))

    lo, hi = own[:, :128], own[:, 128:]
    rate[0] = column(jnp.where(lat == 0, lo, hi))
    rate[1] = column(jnp.where(lat == 0, hi, lo))
    halo = column(jnp.where(lat == 0, other[:, :128], other[:, 128:]))
    rate[2, :RAD] = jnp.where(lat == 0, halo[:RAD], halo[96:])
    near_edge = pl.ds(pl.multiple_of(96 * lat, 32), RAD)
    far_edge = pl.ds(pl.multiple_of(96 * (1 - lat), 32), RAD)
    all_rows = slice(0, HALF)
    halo_rows = slice(HALF, HALF + RAD)
    far_parts = ((0, all_rows, 0, all_rows, 0), (1, near_edge, 1, near_edge, HALF))
    near_parts = (
        (1, all_rows, 1, all_rows, 0),
        (0, far_edge, 0, far_edge, HALF),
        (0, halo_rows, 2, slice(0, RAD), HALF + RAD),
    )
    waves = (far_wave, near_wave)
    varis = (far_vari, near_vari)

    for s in range(SCALES):
        factor = [1.0 / (table[s][0] * table[s][2]), 1.0 / table[s][1] ** 2]
        factor.append(factor[0])
        slot = s % 2
        for parts, span, w, v, tap, var, start in (
            (far_parts, FAR_K, fw, fv, far_tap, far_var, HALF * lat),
            (near_parts, NEAR_K, nw, nv, near_tap, near_var, HALF * (1 - lat)),
        ):
            for source, rows, which, rrows, at in parts:
                size = HALF if at == 0 else RAD
                r = rate[which, rrows, :]
                for j in range(4):
                    cols = slice(128 * j, 128 * j + 128)
                    for k in range(2):
                        t = waves[source][s, k, rows, cols] - r * waves[source][s, 2 + k, rows, cols]
                        high, low = split(t)
                        for copy, t in ((0, high), (1, high), (2, low)):
                            first = span * (2 * copy + k) + at
                            w[slot, first : first + size, cols] = t
                    for k in range(3):
                        t = varis[source][s, k, rows, cols] * (r * factor[k])
                        for copy, t in enumerate(split(t)):
                            first = span * (3 * copy + k) + at
                            v[slot, first : first + size, cols] = t
            wavelet = mm(tap[s], w[slot])
            variance = mm(var[s], v[slot])
            signal = wavelet * lax.rsqrt(jnp.maximum(variance, 1.0))
            there = pl.ds(pl.multiple_of(start, HALF), HALF)
            out[s, there, :] = pltpu.roll(signal, 64, 1)


VMEM = pl.BlockSpec(memory_space=pltpu.VMEM)
ANY = pl.BlockSpec(memory_space=pl.ANY)


def call(kernel, outs, ins, scratch=(), after=(), us=0.01, limit=36):
    count = len(ins)

    def body(*refs):
        kernel(*refs[:count], *refs[count + len(after) :])

    def run(*operands):
        return pl.pallas_call(
            body,
            out_shape=[jax.ShapeDtypeStruct(shape, dtype) for shape, dtype in outs],
            in_specs=list(ins) + [ANY] * len(after),
            out_specs=[VMEM] * len(outs),
            scratch_shapes=list(scratch),
            compiler_params=pltpu.CompilerParams(vmem_limit_bytes=limit * 1024 * 1024),
            cost_estimate=pl.CostEstimate(
                flops=0, bytes_accessed=int(us * 3.6e6), transcendentals=0
            ),
        )(*operands, *after)

    return run


TOKEN = (4, 2 * HALF)
TAPS = [
    ((2, 768, 256 * SCALES), BF16),
    ((2, 512, 384 * SCALES), BF16),
    ((SCALES, HALF, 6 * FAR_K), BF16),
    ((SCALES, HALF, 6 * NEAR_K), BF16),
    ((SCALES, HALF, 6 * FAR_K), BF16),
    ((SCALES, HALF, 6 * NEAR_K), BF16),
]
FINAL_SCRATCH = [pltpu.VMEM((3, HALF, 128), F32)] + [
    pltpu.VMEM((2, 6 * span, TW), BF16) for span in (FAR_K, FAR_K, NEAR_K, NEAR_K)
]


def columns_scratch(rows):
    return [pltpu.VMEM((6 * rows, 768), BF16), pltpu.VMEM((2 * rows, 768), BF16)]


def columns_out(rows):
    return [((SCALES, 4, rows, TW), F32), ((SCALES, 3, rows, TW), F32)]


def per_device(counts_blocks, exposure_blocks, expo_col, expo_count):
    piece = (2, HALF, TW)
    blocks = (4, 2 * HALF, TW)

    def on_lon(value, step):
        return lax.ppermute(value, "lon", [(i, step(i) % LON) for i in range(LON)])

    def two_out(i):
        return i + 2 if i % 2 else i - 2

    def one_out(i):
        return i + 1 if i % 2 else i - 1

    def partner(i):
        return i ^ 1

    inputs = (expo_col, expo_count, counts_blocks, exposure_blocks)
    scalars = [pltpu.SMEM((4,), jnp.int32), pltpu.SMEM((1,), jnp.int32)]
    semaphores = [pltpu.SemaphoreType.DMA((2,)), pltpu.SemaphoreType.DMA((2, 4))]
    (sums,) = call(
        sums_kernel,
        [((2, 2 * HALF), F32)],
        [ANY] * 3,
        [pltpu.VMEM((2, 2 * HALF, 128), F32), scalars[1]]
        + [pltpu.VMEM(blocks, jnp.int32), pltpu.VMEM(blocks, F32)]
        + [pltpu.SemaphoreType.DMA(()), semaphores[1]],
        limit=58,
    )(*inputs[1:])
    sums = sums + on_lon(sums, partner)
    rest = call(
        rest_kernel,
        [(piece, F32)] * 4 + [((2,) + piece, F32)] * 2 + [(TOKEN, F32)],
        [ANY, ANY, VMEM, VMEM],
        [pltpu.VMEM((16, 8, TW), F32)] + scalars + semaphores[:1],
        after=[sums],
        us=3.0,
        limit=24,
    )
    q1n, q1f, q0n, q0f, an, af, rest_token = rest(*inputs)
    an = on_lon(an, partner)
    af = on_lon(af, partner)
    other = lax.ppermute(sums, "lat", [(0, 1), (1, 0)])
    sums = jnp.concatenate([sums, other], axis=0) + rest_token
    far_n, far_f = call(
        far_kernel,
        [(piece, F32), (piece, F32)],
        [ANY, ANY, VMEM, VMEM],
        scalars + semaphores[:1],
        after=[sums],
        us=1.5,
        limit=24,
    )(*inputs)
    b1_n = on_lon(far_n, two_out)
    b1_f = on_lon(far_f, two_out)
    steps = [sums]
    sums = sums + on_lon(sums, lambda i: i ^ 16)
    steps.append(sums)
    ctap, cvar, far_tap, near_tap, far_var, near_var, taps_token = call(
        taps_kernel, TAPS + [(TOKEN, F32)], [], after=[steps[1]], us=3.0
    )()
    for flip in (32, 64, 2):
        sums = sums + on_lon(sums, lambda i: i ^ flip)
        if flip == 64:
            sums = sums + taps_token
        steps.append(sums)

    def merge(after, *pieces):
        return call(
            merge_kernel,
            [(piece, F32), ((2, HALF + 8, TW), F32)],
            [VMEM] * 4,
            after=after,
        )(*pieces)

    def totals(after, *pieces):
        return call(
            total_kernel,
            [(piece, F32), ((2, HALF, 128), F32), ((2, 8, TW), F32)],
            [VMEM] * 3,
            after=after,
        )(*pieces)

    partial_n, sent_n = merge([steps[2]], q1n, q0n, an, b1_n)
    b2_n = on_lon(sent_n, one_out)
    partial_f, sent_f = merge([steps[2]], q1f, q0f, af, b1_f)
    b2_f = on_lon(sent_f, one_out)
    total_n, outer_n, inner_n = totals([steps[3]], partial_n, b2_n, sent_n)
    inner_n = on_lon(inner_n, partner)
    wrap_n, message = call(
        seam_kernel, [((2, HALF, 256), F32), ((2, RAD, TW + 256), F32)], [VMEM] * 3
    )(total_n, outer_n, inner_n)
    lat_rows = lax.ppermute(message, "lat", [(0, 1), (1, 0)])
    near_wave, near_vari, near_token = call(
        near_columns_kernel,
        columns_out(HALF) + [(TOKEN, F32)],
        [VMEM] * 4,
        columns_scratch(HALF),
        us=4.0,
    )(total_n, wrap_n, ctap, cvar)
    sums = sums + near_token
    sums = sums + on_lon(sums, lambda i: i ^ 4)
    last = on_lon(sums, lambda i: i ^ 8)
    total_f, outer_f, inner_f = totals([steps[4]], partial_f, b2_f, sent_f)
    inner_f = on_lon(inner_f, partner)
    far_wave, far_vari = call(
        far_columns_kernel,
        columns_out(HALF + RAD),
        [VMEM] * 6,
        columns_scratch(HALF + RAD),
        us=5.0,
    )(total_f, outer_f, inner_f, lat_rows, ctap, cvar)
    (out,) = call(
        final_kernel, [((SCALES, 2 * HALF, TW), F32)], [VMEM] * 10, FINAL_SCRATCH
    )(near_wave, near_vari, far_wave, far_vari, sums, last, far_tap, near_tap, far_var, near_var)
    return out


def solution(mesh):
    placed = (P("lon", "lat", None), P("lon", "lat", None), P("lon"), P("lon"))
    return jax.shard_map(
        per_device, mesh=mesh, in_specs=placed, out_specs=P(None, "lat", "lon"), check_vma=False
    )
```

```python
import functools

import jax
import jax.numpy as jnp
import ml_dtypes
import numpy as np
from jax import lax
from jax.experimental import pallas as pl
from jax.experimental.pallas import tpu as pltpu
from jax.sharding import PartitionSpec as P

TW = 512
RAD = 32
SCALES = 3
LON = 128
HALF = 128
FAR_K = 160
NEAR_K = 192
F32 = jnp.float32
BF16 = jnp.bfloat16


def iota(shape, dim):
    return lax.broadcasted_iota(jnp.int32, shape, dim)


def where_am_i():
    lon = lax.axis_index("lon")
    return lon, lax.rem(lon, 2), lax.axis_index("lat")


def pack(x):
    lane = iota((8, 128), 1)
    parts = []
    for j in range(4):
        a = x[32 * j : 32 * j + 8]
        for m in range(1, 4):
            b = pltpu.roll(x[32 * j + 8 * m : 32 * j + 8 * m + 8], 32 * m, 1)
            a = jnp.where(lane < 32 * m, a, b)
        parts.append(a)
    return jnp.concatenate(parts, axis=1)


def unpack(p):
    parts = []
    for j in range(4):
        v = p[:, 128 * j : 128 * j + 128]
        parts.append(v)
        for m in range(1, 4):
            parts.append(pltpu.roll(v, 128 - 32 * m, 1))
    return jnp.concatenate(parts, axis=0)


def slot_place(cols, slot, lon):
    column = cols[slot]
    first = column // TW
    within = column - first * TW
    rel = lax.rem(first - lon + LON + LON // 2, LON) - LON // 2
    return within, rel


def fetch_scalars(cols_hbm, count_hbm, cols, count, sem):
    copies = [
        pltpu.make_async_copy(cols_hbm, cols, sem.at[0]),
        pltpu.make_async_copy(count_hbm, count, sem.at[1]),
    ]
    for copy in copies:
        copy.start()
    return copies


def sums_kernel(count_hbm, c_hbm, e_hbm, sums, acc, count, cbuf, ebuf, ssem, sem):
    scalar = pltpu.make_async_copy(count_hbm, count, ssem)
    scalar.start()
    copies = []
    for slot in range(4):
        copies.append(pltpu.make_async_copy(c_hbm.at[slot], cbuf.at[slot], sem.at[0, slot]))
        copies.append(pltpu.make_async_copy(e_hbm.at[slot], ebuf.at[slot], sem.at[1, slot]))
    for copy in copies:
        copy.start()
    acc[...] = jnp.zeros(acc.shape, F32)
    scalar.wait()
    for slot in range(4):
        copies[2 * slot].wait()
        copies[2 * slot + 1].wait()

        @pl.when(slot < count[0])
        def _(slot=slot):
            def body(g, carry):
                rows = pl.ds(pl.multiple_of(8 * g, 8), 8)
                for f, buf in ((0, cbuf), (1, ebuf)):
                    x = buf[slot, rows, :].astype(F32)
                    x = (x[:, :128] + x[:, 128:256]) + (x[:, 256:384] + x[:, 384:])
                    acc[f, rows, :] += x
                return carry

            lax.fori_loop(0, 2 * HALF // 8, body, 0, unroll=8)

    for f in range(2):
        for j in range(2):
            block = jnp.transpose(acc[f, 128 * j : 128 * j + 128, :])
            sums[f : f + 1, 128 * j : 128 * j + 128] = jnp.sum(block, axis=0, keepdims=True)


def far_kernel(cols_hbm, count_hbm, c_hbm, e_hbm, out, cols, count, cbuf, ebuf, ssem, sem):
    lon, core, lat = where_am_i()
    scalars = fetch_scalars(cols_hbm, count_hbm, cols, count, ssem)
    wanted = jnp.where(core == 1, 1, -2)
    for copy in scalars:
        copy.wait()

    def need(slot):
        return jnp.logical_and(slot < count[0], slot_place(cols, slot, lon)[1] == wanted)

    def loads(slot):
        return (
            pltpu.make_async_copy(c_hbm.at[slot], cbuf.at[slot], sem.at[0, slot]),
            pltpu.make_async_copy(e_hbm.at[slot], ebuf.at[slot], sem.at[1, slot]),
        )

    for slot in range(4):

        @pl.when(need(slot))
        def _(slot=slot):
            for load in loads(slot):
                load.start()

    out[...] = jnp.zeros(out.shape, F32)
    for slot in range(4):

        @pl.when(need(slot))
        def _(slot=slot):
            for load in loads(slot):
                load.wait()
            within, _ = slot_place(cols, slot, lon)
            lane = iota((8, 128), 1)

            for first, start in ((0, HALF * (1 - lat)), (HALF, HALF * lat)):

                def body(g, carry, first=first, start=start):
                    rows = pl.ds(pl.multiple_of(start + 8 * g, 8), 8)
                    here = pl.ds(pl.multiple_of(first + 8 * g, 8), 8)
                    for f, buf in ((0, cbuf), (1, ebuf)):
                        x = rolled(buf, slot, rows, within)
                        for j in range(4):
                            col = lane + 128 * j
                            keep = jnp.where(core == 1, col - within, within - 1 - col) < 0
                            out[f, here, 128 * j : 128 * j + 128] += jnp.where(keep, x[j], 0.0)
                    return carry

                lax.fori_loop(0, HALF // 8, body, 0, unroll=4)


def rolled(buf, slot, rows, within):
    whole = within // 128
    rest = within - 128 * whole
    first = iota((8, 128), 1) < rest
    turned = []
    for j in range(4):
        block = lax.rem(j + 4 - whole, 4)
        x = buf[slot, rows, pl.ds(pl.multiple_of(128 * block, 128), 128)].astype(F32)
        turned.append(pltpu.roll(x, rest, 1))
    return [jnp.where(first, turned[j - 1], turned[j]) for j in range(4)]


def rest_kernel(
    cols_hbm, count_hbm, cbuf, ebuf, q1n, q1f, q0n, q0f, an, af, token, weight, cols, count, ssem
):
    lon, core, lat = where_am_i()
    for copy in fetch_scalars(cols_hbm, count_hbm, cols, count, ssem):
        copy.wait()
    token[...] = jnp.zeros(token.shape, F32)
    sign = 2 * core - 1
    col = iota((8, TW), 1)
    shifts = []
    for slot in range(4):
        within, rel = slot_place(cols, slot, lon)
        alive = slot < count[0]
        shifts.append(within)
        for k, q in enumerate((1, 0, -1, -2)):
            high = jnp.where(jnp.logical_and(alive, rel * sign == q), 1.0, 0.0).astype(F32)
            low = jnp.where(jnp.logical_and(alive, (rel + 1) * sign == q), 1.0, 0.0).astype(F32)
            weight[4 * slot + k] = jnp.where(col >= within, high, low)
    for q1, q0, a, start in ((q1n, q0n, an, HALF * (1 - lat)), (q1f, q0f, af, HALF * lat)):

        def body(g, carry, q1=q1, q0=q0, a=a, start=start):
            rows = pl.ds(pl.multiple_of(start + 8 * g, 8), 8)
            here = pl.ds(pl.multiple_of(8 * g, 8), 8)
            for f, buf in ((0, cbuf), (1, ebuf)):
                xs = [rolled(buf, slot, rows, shifts[slot]) for slot in range(4)]
                for j in range(4):
                    block = slice(128 * j, 128 * j + 128)
                    outs = (q1.at[f], q0.at[f], a.at[0, f], a.at[1, f])
                    for k, out in enumerate(outs):
                        t = xs[0][j] * weight[k, :, block]
                        for slot in range(1, 4):
                            t = t + xs[slot][j] * weight[4 * slot + k, :, block]
                        out[here, block] = t
            return carry

        lax.fori_loop(0, HALF // 8, body, 0, unroll=4)


def token_kernel(arrived, token):
    token[...] = jnp.zeros(token.shape, F32)


def merge_kernel(first, q1, q0, a, b1, partial, message):
    _, core, _ = where_am_i()
    for f in range(2):
        message[f, :HALF, :] = q1[f] + a[1, f]
        mine = q0[f] + a[0, f] + b1[f, first : first + HALF, :]
        partial[f] = mine
        edge = jnp.where(core == 1, pltpu.roll(mine[:, 384:], 32, 1), mine[:, :128])
        message[f, HALF:, :] = pack(edge)


def total_kernel(partial, received, sent, total, outer, inner):
    _, core, _ = where_am_i()
    for f in range(2):
        mine = partial[f] + received[f, :HALF, :]
        total[f] = mine
        near = jnp.where(
            core == 1, sent[f, :HALF, :128], pltpu.roll(sent[f, :HALF, 384:], 32, 1)
        )
        outer[f] = unpack(received[f, HALF:, :]) + near
        edge = jnp.where(core == 1, mine[:, :128], pltpu.roll(mine[:, 384:], 32, 1))
        inner[f] = pack(edge)


def seam(total, outer, inner, core):
    lane = iota((HALF, 128), 1)
    left = jnp.where(core == 1, inner, outer)
    right = jnp.where(core == 1, outer, inner)
    a = jnp.where(lane < 96, pltpu.roll(total[:, 384:], 96, 1), pltpu.roll(right, 96, 1))
    b = jnp.where(lane < 32, left, pltpu.roll(total[:, :128], 32, 1))
    return jnp.concatenate([a, b], axis=1)


def seam_kernel(total, outer, inner, wrap, message):
    _, core, lat = where_am_i()
    rows = pl.ds(pl.multiple_of(96 * (1 - lat), 32), 32)
    for f in range(2):
        wrap[f] = seam(total[f], outer[f], unpack(inner[f]), core)
        message[f, :, :TW] = total[f, rows, :]
        message[f, :, TW:] = wrap[f, rows, :]


def bell_hat(offset, sigma):
    inside = jnp.abs(offset) <= RAD
    d = offset.astype(F32)
    bell = jnp.where(inside, jnp.exp(-d * d / (2.0 * sigma * sigma)), 0.0)
    hat = (1.0 - d * d / (sigma * sigma)) * bell
    return bell, hat


def split(x):
    high = x.astype(BF16)
    return high, (x - high.astype(F32)).astype(BF16)


@functools.cache
def tap_scales():
    t = np.arange(-RAD, RAD + 1, dtype=np.float64)
    table = []
    for s in range(SCALES):
        sigma = RAD / 2.0 ** (4 - s)
        g = np.exp(-t * t / (2.0 * sigma * sigma))
        h = (1.0 - t * t / (sigma * sigma)) * g
        row = []
        for k in (h * h, h * g, g * g):
            c = 1.0 + np.arange(4096) / 4096.0
            error = (k * c[:, None]).astype(ml_dtypes.bfloat16).astype(np.float64) / c[:, None] - k
            cost = np.abs(error.sum(1)) / np.abs(k).sum()
            cost = 4.0 * cost + np.sqrt((error**2).sum(1) / (k**2).sum())
            row.append(float(c[np.argmin(cost)]))
        table.append(row)
    return table


def taps_kernel(ctap, cvar, far_tap, near_tap, far_var, near_var, token):
    _, _, lat = where_am_i()
    token[...] = jnp.zeros(token.shape, F32)
    w = iota((256, 128), 0)
    n = iota((256, 128), 1)
    straight = w - n - 64
    wrapped_w = jnp.where(w < 128, 416 + w, w - 160)
    wrapped_n = jnp.where(n < 64, 448 + n, n - 64)
    a = iota((HALF, 128), 0)
    b = iota((HALF, 128), 1)
    table = tap_scales()

    def far_row(p):
        return jnp.where(lat == 0, p, jnp.where(p < HALF, p + HALF, p - 32))

    def near_row(p):
        inner = jnp.where(lat == 0, p + HALF, p)
        adjacent = jnp.where(lat == 0, p - 32, p)
        halo = jnp.where(lat == 0, p + 96, p - 192)
        return jnp.where(p < HALF, inner, jnp.where(p < HALF + 32, adjacent, halo))

    for s in range(SCALES):
        sigma = RAD / 2.0 ** (4 - s)
        chh, chg, cgg = table[s]
        for kind, offset in ((0, straight), (1, wrapped_w - wrapped_n)):
            bell, hat = bell_hat(offset, sigma)
            for k, t in enumerate((hat, bell)):
                high, low = split(t)
                here = slice(256 * s + 128 * k, 256 * s + 128 * k + 128)
                ctap[kind, :256, here] = high
                ctap[kind, 256:512, here] = high
                ctap[kind, 512:, here] = low
            for k, t in enumerate((chh * hat * hat, chg * hat * bell, cgg * bell * bell)):
                here = slice(384 * s + 128 * k, 384 * s + 128 * k + 128)
                t = t.astype(BF16)
                cvar[kind, :256, here] = t
                cvar[kind, 256:, here] = t
        for tap, var, span, place in (
            (far_tap, far_var, FAR_K, far_row),
            (near_tap, near_var, NEAR_K, near_row),
        ):
            for j in range(-(-6 * span // 128)):
                here = slice(128 * j, min(128 * j + 128, 6 * span))
                size = here.stop - here.start
                lane = 128 * j + b
                copy = (lane >= 2 * span).astype(jnp.int32) + (lane >= 4 * span).astype(jnp.int32)
                p = lane - 2 * span * copy
                second = p >= span
                bell, hat = bell_hat(place(jnp.where(second, p - span, p)) - place(a), sigma)
                high, low = split(jnp.where(second, hat, bell))
                t = jnp.where(copy == 1, low.astype(F32), high.astype(F32)).astype(BF16)
                tap[s, :, here] = t[:, :size]
                p = jnp.where(lane >= 3 * span, lane - 3 * span, lane)
                which = (p >= span).astype(jnp.int32) + (p >= 2 * span).astype(jnp.int32)
                bell, hat = bell_hat(place(p - span * which) - place(a), sigma)
                t = jnp.where(which == 1, (2.0 * chg) * hat * bell, chh * hat * hat)
                t = jnp.where(which == 0, cgg * bell * bell, t).astype(BF16)
                var[s, :, here] = t[:, :size]


def mm(a, b):
    return jnp.dot(a, b, preferred_element_type=F32)


def column_filters(size, fields, ctap, cvar, wave, vari, x, xw):
    for j in range(6):
        for f in range(2):
            high, low = split(fields(f, j))
            if j < 4:
                places = [(x, 3 * f + b, j - b) for b in range(3) if j - b in (0, 1)]
            else:
                places = [(xw, f, j - 4)]
            for ref, b, side in places:
                rows = slice(size * b, size * b + size)
                ref[rows, 128 * side : 128 * side + 128] = high
                ref[rows, 256 + 128 * side : 384 + 128 * side] = low
                ref[rows, 512 + 128 * side : 640 + 128 * side] = high
    for f in range(2):
        y = mm(x[3 * size * f : 3 * size * (f + 1), :], ctap[0])
        for s in range(SCALES):
            for k in range(2):
                for b in range(3):
                    wave[s, 2 * f + k, :, 128 * b : 128 * b + 128] = y[
                        size * b : size * b + size, 256 * s + 128 * k : 256 * s + 128 * k + 128
                    ]
    z = mm(x[3 * size :, :512], cvar[0])
    for s in range(SCALES):
        for k in range(3):
            for b in range(3):
                vari[s, k, :, 128 * b : 128 * b + 128] = z[
                    size * b : size * b + size, 384 * s + 128 * k : 384 * s + 128 * k + 128
                ]
    y = mm(xw[...], ctap[1])
    z = mm(xw[size:, :512], cvar[1])
    for s in range(SCALES):
        for k in range(2):
            here = slice(256 * s + 128 * k, 256 * s + 128 * k + 128)
            wave[s, k, :, 384:] = y[:size, here]
            wave[s, 2 + k, :, 384:] = y[size:, here]
        for k in range(3):
            vari[s, k, :, 384:] = z[:, 384 * s + 128 * k : 384 * s + 128 * k + 128]


def near_columns_kernel(total, wrap, ctap, cvar, wave, vari, token, x, xw):
    token[...] = jnp.zeros(token.shape, F32)

    def fields(f, j):
        if j < 4:
            return total[f, :, 128 * j : 128 * j + 128]
        return wrap[f, :, 128 * (j - 4) : 128 * (j - 3)]

    column_filters(HALF, fields, ctap, cvar, wave, vari, x, xw)


def far_columns_kernel(total, outer, inner, lat_rows, ctap, cvar, wave, vari, x, xw):
    _, core, _ = where_am_i()
    wrap = [seam(total[f], outer[f], unpack(inner[f]), core) for f in range(2)]

    def fields(f, j):
        if j < 4:
            mine = total[f, :, 128 * j : 128 * j + 128]
        else:
            mine = wrap[f][:, 128 * (j - 4) : 128 * (j - 3)]
        return jnp.concatenate([mine, lat_rows[f, :, 128 * j : 128 * j + 128]], axis=0)

    column_filters(HALF + RAD, fields, ctap, cvar, wave, vari, x, xw)


def final_kernel(
    near_wave, near_vari, far_wave, far_vari, sums, last,
    far_tap, near_tap, far_var, near_var, out, rate, fw, fv, nw, nv,
):
    _, core, lat = where_am_i()
    whole = sums[...] + last[...]
    own = whole[0:1] / whole[1:2]
    other = whole[2:3] / whole[3:4]
    table = tap_scales()

    def column(row):
        return jnp.transpose(jnp.broadcast_to(row, (128, 128)))

    lo, hi = own[:, :128], own[:, 128:]
    rate[0] = column(jnp.where(lat == 0, lo, hi))
    rate[1] = column(jnp.where(lat == 0, hi, lo))
    halo = column(jnp.where(lat == 0, other[:, :128], other[:, 128:]))
    rate[2, :RAD] = jnp.where(lat == 0, halo[:RAD], halo[96:])
    near_edge = pl.ds(pl.multiple_of(96 * lat, 32), RAD)
    far_edge = pl.ds(pl.multiple_of(96 * (1 - lat), 32), RAD)
    all_rows = slice(0, HALF)
    halo_rows = slice(HALF, HALF + RAD)
    far_parts = ((0, all_rows, 0, all_rows, 0), (1, near_edge, 1, near_edge, HALF))
    near_parts = (
        (1, all_rows, 1, all_rows, 0),
        (0, far_edge, 0, far_edge, HALF),
        (0, halo_rows, 2, slice(0, RAD), HALF + RAD),
    )
    waves = (far_wave, near_wave)
    varis = (far_vari, near_vari)

    def prepare(s):
        factor = [1.0 / (table[s][0] * table[s][2]), 1.0 / table[s][1] ** 2]
        factor.append(factor[0])
        slot = s
        for parts, span, w, v in ((far_parts, FAR_K, fw, fv), (near_parts, NEAR_K, nw, nv)):
            for source, rows, which, rrows, at in parts:
                size = HALF if at == 0 else RAD
                r = rate[which, rrows, :]
                for j in range(4):
                    cols = slice(128 * j, 128 * j + 128)
                    for k in range(2):
                        t = waves[source][s, k, rows, cols] - r * waves[source][s, 2 + k, rows, cols]
                        high, low = split(t)
                        for copy, t in ((0, high), (1, high), (2, low)):
                            first = span * (2 * copy + k) + at
                            w[slot, first : first + size, cols] = t
                    for k in range(3):
                        t = varis[source][s, k, rows, cols] * (r * factor[k])
                        for copy, t in enumerate(split(t)):
                            first = span * (3 * copy + k) + at
                            v[slot, first : first + size, cols] = t

    def multiply(s):
        slot = s
        for w, v, tap, var, start in (
            (fw, fv, far_tap, far_var, HALF * lat),
            (nw, nv, near_tap, near_var, HALF * (1 - lat)),
        ):
            wavelet = mm(tap[s], w[slot])
            variance = mm(var[s], v[slot])
            signal = wavelet * lax.rsqrt(jnp.maximum(variance, 1.0))
            there = pl.ds(pl.multiple_of(start, HALF), HALF)
            out[s, there, :] = pltpu.roll(signal, 64, 1)

    @pl.when(lat >= 0)
    def _():
        for s in range(SCALES):
            prepare(s)

    @pl.when(lat >= 0)
    def _():
        for s in range(SCALES):
            multiply(s)


VMEM = pl.BlockSpec(memory_space=pltpu.VMEM)
ANY = pl.BlockSpec(memory_space=pl.ANY)


def call(kernel, outs, ins, scratch=(), after=(), us=0.01, limit=36):
    count = len(ins)

    def body(*refs):
        kernel(*refs[:count], *refs[count + len(after) :])

    def run(*operands):
        return pl.pallas_call(
            body,
            out_shape=[jax.ShapeDtypeStruct(shape, dtype) for shape, dtype in outs],
            in_specs=list(ins) + [ANY] * len(after),
            out_specs=[VMEM] * len(outs),
            scratch_shapes=list(scratch),
            compiler_params=pltpu.CompilerParams(vmem_limit_bytes=limit * 1024 * 1024),
            cost_estimate=pl.CostEstimate(
                flops=0, bytes_accessed=int(us * 3.6e6), transcendentals=0
            ),
        )(*operands, *after)

    return run


TOKEN = (4, 2 * HALF)
TAPS = [
    ((2, 768, 256 * SCALES), BF16),
    ((2, 512, 384 * SCALES), BF16),
    ((SCALES, HALF, 6 * FAR_K), BF16),
    ((SCALES, HALF, 6 * NEAR_K), BF16),
    ((SCALES, HALF, 6 * FAR_K), BF16),
    ((SCALES, HALF, 6 * NEAR_K), BF16),
]
FINAL_SCRATCH = [pltpu.VMEM((3, HALF, 128), F32)] + [
    pltpu.VMEM((SCALES, 6 * span, TW), BF16) for span in (FAR_K, FAR_K, NEAR_K, NEAR_K)
]


def columns_scratch(rows):
    return [pltpu.VMEM((6 * rows, 768), BF16), pltpu.VMEM((2 * rows, 768), BF16)]


def columns_out(rows):
    return [((SCALES, 4, rows, TW), F32), ((SCALES, 3, rows, TW), F32)]


def per_device(counts_blocks, exposure_blocks, expo_col, expo_count):
    piece = (2, HALF, TW)
    blocks = (4, 2 * HALF, TW)

    def on_lon(value, step):
        return lax.ppermute(value, "lon", [(i, step(i) % LON) for i in range(LON)])

    def two_out(i):
        return i + 2 if i % 2 else i - 2

    def one_out(i):
        return i + 1 if i % 2 else i - 1

    def partner(i):
        return i ^ 1

    inputs = (expo_col, expo_count, counts_blocks, exposure_blocks)
    scalars = [pltpu.SMEM((4,), jnp.int32), pltpu.SMEM((1,), jnp.int32)]
    semaphores = [pltpu.SemaphoreType.DMA((2,)), pltpu.SemaphoreType.DMA((2, 4))]
    (sums,) = call(
        sums_kernel,
        [((2, 2 * HALF), F32)],
        [ANY] * 3,
        [pltpu.VMEM((2, 2 * HALF, 128), F32), scalars[1]]
        + [pltpu.VMEM(blocks, jnp.int32), pltpu.VMEM(blocks, F32)]
        + [pltpu.SemaphoreType.DMA(()), semaphores[1]],
        limit=58,
    )(*inputs[1:])
    sums = sums + on_lon(sums, partner)
    rest = call(
        rest_kernel,
        [(piece, F32)] * 4 + [((2,) + piece, F32)] * 2 + [(TOKEN, F32)],
        [ANY, ANY, VMEM, VMEM],
        [pltpu.VMEM((16, 8, TW), F32)] + scalars + semaphores[:1],
        after=[sums],
        us=3.0,
        limit=24,
    )
    q1n, q1f, q0n, q0f, an, af, rest_token = rest(*inputs)
    an = on_lon(an, partner)
    af = on_lon(af, partner)
    other = lax.ppermute(sums, "lat", [(0, 1), (1, 0)])
    sums = jnp.concatenate([sums, other], axis=0) + rest_token
    (b1,) = call(
        far_kernel,
        [((2, 2 * HALF, TW), F32)],
        [ANY] * 4,
        scalars + [pltpu.VMEM(blocks, jnp.int32), pltpu.VMEM(blocks, F32)] + semaphores,
        limit=58,
    )(*inputs)
    b1 = on_lon(b1, two_out)
    steps = [sums]
    (b1_token,) = call(token_kernel, [(TOKEN, F32)], [ANY])(b1)
    sums = sums + on_lon(sums, lambda i: i ^ 16)
    steps.append(sums + b1_token)
    ctap, cvar, far_tap, near_tap, far_var, near_var, taps_token = call(
        taps_kernel, TAPS + [(TOKEN, F32)], [], after=[steps[1]], us=3.0
    )()
    sums = steps[1]
    for flip in (32, 64, 2):
        sums = sums + on_lon(sums, lambda i: i ^ flip)
        if flip == 64:
            sums = sums + taps_token
        steps.append(sums)

    def merge(first, after, *pieces):
        return call(
            functools.partial(merge_kernel, first),
            [(piece, F32), ((2, HALF + 8, TW), F32)],
            [VMEM] * 4,
            after=after,
        )(*pieces)

    def totals(after, *pieces):
        return call(
            total_kernel,
            [(piece, F32), ((2, HALF, 128), F32), ((2, 8, TW), F32)],
            [VMEM] * 3,
            after=after,
        )(*pieces)

    partial_n, sent_n = merge(0, [steps[1]], q1n, q0n, an, b1)
    b2_n = on_lon(sent_n, one_out)
    partial_f, sent_f = merge(HALF, [steps[1]], q1f, q0f, af, b1)
    b2_f = on_lon(sent_f, one_out)
    total_n, outer_n, inner_n = totals([steps[3]], partial_n, b2_n, sent_n)
    inner_n = on_lon(inner_n, partner)
    wrap_n, message = call(
        seam_kernel, [((2, HALF, 256), F32), ((2, RAD, TW + 256), F32)], [VMEM] * 3
    )(total_n, outer_n, inner_n)
    lat_rows = lax.ppermute(message, "lat", [(0, 1), (1, 0)])
    near_wave, near_vari, near_token = call(
        near_columns_kernel,
        columns_out(HALF) + [(TOKEN, F32)],
        [VMEM] * 4,
        columns_scratch(HALF),
        us=4.0,
    )(total_n, wrap_n, ctap, cvar)
    sums = sums + near_token
    sums = sums + on_lon(sums, lambda i: i ^ 4)
    last = on_lon(sums, lambda i: i ^ 8)
    total_f, outer_f, inner_f = totals([steps[4]], partial_f, b2_f, sent_f)
    inner_f = on_lon(inner_f, partner)
    far_wave, far_vari = call(
        far_columns_kernel,
        columns_out(HALF + RAD),
        [VMEM] * 6,
        columns_scratch(HALF + RAD),
        us=5.0,
    )(total_f, outer_f, inner_f, lat_rows, ctap, cvar)
    (out,) = call(
        final_kernel, [((SCALES, 2 * HALF, TW), F32)], [VMEM] * 10, FINAL_SCRATCH
    )(near_wave, near_vari, far_wave, far_vari, sums, last, far_tap, near_tap, far_var, near_var)
    return out


def solution(mesh):
    placed = (P("lon", "lat", None), P("lon", "lat", None), P("lon"), P("lon"))
    return jax.shard_map(
        per_device, mesh=mesh, in_specs=placed, out_specs=P(None, "lat", "lon"), check_vma=False
    )
```

```python
import functools

import jax
import jax.numpy as jnp
import ml_dtypes
import numpy as np
from jax import lax
from jax.experimental import pallas as pl
from jax.experimental.pallas import tpu as pltpu
from jax.sharding import PartitionSpec as P

TW = 512
RAD = 32
SCALES = 3
LON = 128
HALF = 128
FAR_K = 160
NEAR_K = 192
F32 = jnp.float32
BF16 = jnp.bfloat16


def iota(shape, dim):
    return lax.broadcasted_iota(jnp.int32, shape, dim)


def where_am_i():
    lon = lax.axis_index("lon")
    return lon, lax.rem(lon, 2), lax.axis_index("lat")


def pack(x):
    lane = iota((8, 128), 1)
    parts = []
    for j in range(4):
        a = x[32 * j : 32 * j + 8]
        for m in range(1, 4):
            b = pltpu.roll(x[32 * j + 8 * m : 32 * j + 8 * m + 8], 32 * m, 1)
            a = jnp.where(lane < 32 * m, a, b)
        parts.append(a)
    return jnp.concatenate(parts, axis=1)


def unpack(p):
    parts = []
    for j in range(4):
        v = p[:, 128 * j : 128 * j + 128]
        parts.append(v)
        for m in range(1, 4):
            parts.append(pltpu.roll(v, 128 - 32 * m, 1))
    return jnp.concatenate(parts, axis=0)


def slot_place(cols, slot, lon):
    column = cols[slot]
    first = column // TW
    within = column - first * TW
    rel = lax.rem(first - lon + LON + LON // 2, LON) - LON // 2
    return within, rel


def fetch_scalars(cols_hbm, count_hbm, cols, count, sem):
    copies = [
        pltpu.make_async_copy(cols_hbm, cols, sem.at[0]),
        pltpu.make_async_copy(count_hbm, count, sem.at[1]),
    ]
    for copy in copies:
        copy.start()
    return copies


def first_kernel(
    cols_hbm, count_hbm, c_hbm, e_hbm, out, sums, acc, cols, count, cbuf, ebuf, ssem, sem
):
    lon, core, lat = where_am_i()
    scalars = fetch_scalars(cols_hbm, count_hbm, cols, count, ssem)
    copies = []
    for slot in range(4):
        copies.append(pltpu.make_async_copy(c_hbm.at[slot], cbuf.at[slot], sem.at[0, slot]))
        copies.append(pltpu.make_async_copy(e_hbm.at[slot], ebuf.at[slot], sem.at[1, slot]))
    for copy in copies:
        copy.start()
    wanted = jnp.where(core == 1, 1, -2)
    out[...] = jnp.zeros(out.shape, F32)
    acc[...] = jnp.zeros(acc.shape, F32)
    for copy in scalars:
        copy.wait()
    for slot in range(4):
        copies[2 * slot].wait()
        copies[2 * slot + 1].wait()

        @pl.when(slot < count[0])
        def _(slot=slot):
            def body(g, carry):
                rows = pl.ds(pl.multiple_of(8 * g, 8), 8)
                for f, buf in ((0, cbuf), (1, ebuf)):
                    x = buf[slot, rows, :].astype(F32)
                    x = (x[:, :128] + x[:, 128:256]) + (x[:, 256:384] + x[:, 384:])
                    acc[f, rows, :] += x
                return carry

            lax.fori_loop(0, 2 * HALF // 8, body, 0, unroll=8)

        within, rel = slot_place(cols, slot, lon)

        @pl.when(jnp.logical_and(slot < count[0], rel == wanted))
        def _(slot=slot, within=within):
            lane = iota((8, 128), 1)

            for first, start in ((0, HALF * (1 - lat)), (HALF, HALF * lat)):

                def body(g, carry, first=first, start=start):
                    rows = pl.ds(pl.multiple_of(start + 8 * g, 8), 8)
                    here = pl.ds(pl.multiple_of(first + 8 * g, 8), 8)
                    for f, buf in ((0, cbuf), (1, ebuf)):
                        x = rolled(buf, slot, rows, within)
                        for j in range(4):
                            col = lane + 128 * j
                            keep = jnp.where(core == 1, col - within, within - 1 - col) < 0
                            out[f, here, 128 * j : 128 * j + 128] += jnp.where(keep, x[j], 0.0)
                    return carry

                lax.fori_loop(0, HALF // 8, body, 0, unroll=4)

    for f in range(2):
        for j in range(2):
            block = jnp.transpose(acc[f, 128 * j : 128 * j + 128, :])
            sums[f : f + 1, 128 * j : 128 * j + 128] = jnp.sum(block, axis=0, keepdims=True)


def rolled(buf, slot, rows, within):
    whole = within // 128
    rest = within - 128 * whole
    first = iota((8, 128), 1) < rest
    turned = []
    for j in range(4):
        block = lax.rem(j + 4 - whole, 4)
        x = buf[slot, rows, pl.ds(pl.multiple_of(128 * block, 128), 128)].astype(F32)
        turned.append(pltpu.roll(x, rest, 1))
    return [jnp.where(first, turned[j - 1], turned[j]) for j in range(4)]


def rest_kernel(
    cols_hbm, count_hbm, cbuf, ebuf, q1n, q1f, q0n, q0f, an, af, token, weight, cols, count, ssem
):
    lon, core, lat = where_am_i()
    for copy in fetch_scalars(cols_hbm, count_hbm, cols, count, ssem):
        copy.wait()
    token[...] = jnp.zeros(token.shape, F32)
    sign = 2 * core - 1
    col = iota((8, TW), 1)
    shifts = []
    for slot in range(4):
        within, rel = slot_place(cols, slot, lon)
        alive = slot < count[0]
        shifts.append(within)
        for k, q in enumerate((1, 0, -1, -2)):
            high = jnp.where(jnp.logical_and(alive, rel * sign == q), 1.0, 0.0).astype(F32)
            low = jnp.where(jnp.logical_and(alive, (rel + 1) * sign == q), 1.0, 0.0).astype(F32)
            weight[4 * slot + k] = jnp.where(col >= within, high, low)
    for q1, q0, a, start in ((q1n, q0n, an, HALF * (1 - lat)), (q1f, q0f, af, HALF * lat)):

        def body(g, carry, q1=q1, q0=q0, a=a, start=start):
            rows = pl.ds(pl.multiple_of(start + 8 * g, 8), 8)
            here = pl.ds(pl.multiple_of(8 * g, 8), 8)
            for f, buf in ((0, cbuf), (1, ebuf)):
                xs = [rolled(buf, slot, rows, shifts[slot]) for slot in range(4)]
                for j in range(4):
                    block = slice(128 * j, 128 * j + 128)
                    outs = (q1.at[f], q0.at[f], a.at[0, f], a.at[1, f])
                    for k, out in enumerate(outs):
                        t = xs[0][j] * weight[k, :, block]
                        for slot in range(1, 4):
                            t = t + xs[slot][j] * weight[4 * slot + k, :, block]
                        out[here, block] = t
            return carry

        lax.fori_loop(0, HALF // 8, body, 0, unroll=4)


def token_kernel(arrived, token):
    token[...] = jnp.zeros(token.shape, F32)


def merge_kernel(first, q1, q0, a, b1, partial, message):
    _, core, _ = where_am_i()
    for f in range(2):
        message[f, :HALF, :] = q1[f] + a[1, f]
        mine = q0[f] + a[0, f] + b1[f, first : first + HALF, :]
        partial[f] = mine
        edge = jnp.where(core == 1, pltpu.roll(mine[:, 384:], 32, 1), mine[:, :128])
        message[f, HALF:, :] = pack(edge)


def total_kernel(partial, received, sent, total, outer, inner):
    _, core, _ = where_am_i()
    for f in range(2):
        mine = partial[f] + received[f, :HALF, :]
        total[f] = mine
        near = jnp.where(
            core == 1, sent[f, :HALF, :128], pltpu.roll(sent[f, :HALF, 384:], 32, 1)
        )
        outer[f] = unpack(received[f, HALF:, :]) + near
        edge = jnp.where(core == 1, mine[:, :128], pltpu.roll(mine[:, 384:], 32, 1))
        inner[f] = pack(edge)


def seam(total, outer, inner, core):
    lane = iota((HALF, 128), 1)
    left = jnp.where(core == 1, inner, outer)
    right = jnp.where(core == 1, outer, inner)
    a = jnp.where(lane < 96, pltpu.roll(total[:, 384:], 96, 1), pltpu.roll(right, 96, 1))
    b = jnp.where(lane < 32, left, pltpu.roll(total[:, :128], 32, 1))
    return jnp.concatenate([a, b], axis=1)


def seam_kernel(total, outer, inner, wrap, message):
    _, core, lat = where_am_i()
    rows = pl.ds(pl.multiple_of(96 * (1 - lat), 32), 32)
    for f in range(2):
        wrap[f] = seam(total[f], outer[f], unpack(inner[f]), core)
        message[f, :, :TW] = total[f, rows, :]
        message[f, :, TW:] = wrap[f, rows, :]


def bell_hat(offset, sigma):
    inside = jnp.abs(offset) <= RAD
    d = offset.astype(F32)
    bell = jnp.where(inside, jnp.exp(-d * d / (2.0 * sigma * sigma)), 0.0)
    hat = (1.0 - d * d / (sigma * sigma)) * bell
    return bell, hat


def split(x):
    high = x.astype(BF16)
    return high, (x - high.astype(F32)).astype(BF16)


@functools.cache
def tap_scales():
    t = np.arange(-RAD, RAD + 1, dtype=np.float64)
    table = []
    for s in range(SCALES):
        sigma = RAD / 2.0 ** (4 - s)
        g = np.exp(-t * t / (2.0 * sigma * sigma))
        h = (1.0 - t * t / (sigma * sigma)) * g
        row = []
        for k in (h * h, h * g, g * g):
            c = 1.0 + np.arange(4096) / 4096.0
            error = (k * c[:, None]).astype(ml_dtypes.bfloat16).astype(np.float64) / c[:, None] - k
            cost = np.abs(error.sum(1)) / np.abs(k).sum()
            cost = 4.0 * cost + np.sqrt((error**2).sum(1) / (k**2).sum())
            row.append(float(c[np.argmin(cost)]))
        table.append(row)
    return table


def taps_kernel(ctap, cvar, far_tap, near_tap, far_var, near_var, token):
    _, _, lat = where_am_i()
    token[...] = jnp.zeros(token.shape, F32)
    w = iota((256, 128), 0)
    n = iota((256, 128), 1)
    straight = w - n - 64
    wrapped_w = jnp.where(w < 128, 416 + w, w - 160)
    wrapped_n = jnp.where(n < 64, 448 + n, n - 64)
    a = iota((HALF, 128), 0)
    b = iota((HALF, 128), 1)
    table = tap_scales()

    def far_row(p):
        return jnp.where(lat == 0, p, jnp.where(p < HALF, p + HALF, p - 32))

    def near_row(p):
        inner = jnp.where(lat == 0, p + HALF, p)
        adjacent = jnp.where(lat == 0, p - 32, p)
        halo = jnp.where(lat == 0, p + 96, p - 192)
        return jnp.where(p < HALF, inner, jnp.where(p < HALF + 32, adjacent, halo))

    for s in range(SCALES):
        sigma = RAD / 2.0 ** (4 - s)
        chh, chg, cgg = table[s]
        for kind, offset in ((0, straight), (1, wrapped_w - wrapped_n)):
            bell, hat = bell_hat(offset, sigma)
            for k, t in enumerate((hat, bell)):
                high, low = split(t)
                here = slice(256 * s + 128 * k, 256 * s + 128 * k + 128)
                ctap[kind, :256, here] = high
                ctap[kind, 256:512, here] = high
                ctap[kind, 512:, here] = low
            for k, t in enumerate((chh * hat * hat, chg * hat * bell, cgg * bell * bell)):
                here = slice(384 * s + 128 * k, 384 * s + 128 * k + 128)
                t = t.astype(BF16)
                cvar[kind, :256, here] = t
                cvar[kind, 256:, here] = t
        for tap, var, span, place in (
            (far_tap, far_var, FAR_K, far_row),
            (near_tap, near_var, NEAR_K, near_row),
        ):
            for j in range(-(-6 * span // 128)):
                here = slice(128 * j, min(128 * j + 128, 6 * span))
                size = here.stop - here.start
                lane = 128 * j + b
                copy = (lane >= 2 * span).astype(jnp.int32) + (lane >= 4 * span).astype(jnp.int32)
                p = lane - 2 * span * copy
                second = p >= span
                bell, hat = bell_hat(place(jnp.where(second, p - span, p)) - place(a), sigma)
                high, low = split(jnp.where(second, hat, bell))
                t = jnp.where(copy == 1, low.astype(F32), high.astype(F32)).astype(BF16)
                tap[s, :, here] = t[:, :size]
                p = jnp.where(lane >= 3 * span, lane - 3 * span, lane)
                which = (p >= span).astype(jnp.int32) + (p >= 2 * span).astype(jnp.int32)
                bell, hat = bell_hat(place(p - span * which) - place(a), sigma)
                t = jnp.where(which == 1, (2.0 * chg) * hat * bell, chh * hat * hat)
                t = jnp.where(which == 0, cgg * bell * bell, t).astype(BF16)
                var[s, :, here] = t[:, :size]


def mm(a, b):
    return jnp.dot(a, b, preferred_element_type=F32)


def column_filters(size, fields, ctap, cvar, wave, vari, x, xw):
    for j in range(6):
        for f in range(2):
            high, low = split(fields(f, j))
            if j < 4:
                places = [(x, 3 * f + b, j - b) for b in range(3) if j - b in (0, 1)]
            else:
                places = [(xw, f, j - 4)]
            for ref, b, side in places:
                rows = slice(size * b, size * b + size)
                ref[rows, 128 * side : 128 * side + 128] = high
                ref[rows, 256 + 128 * side : 384 + 128 * side] = low
                ref[rows, 512 + 128 * side : 640 + 128 * side] = high
    for f in range(2):
        y = mm(x[3 * size * f : 3 * size * (f + 1), :], ctap[0])
        for s in range(SCALES):
            for k in range(2):
                for b in range(3):
                    wave[s, 2 * f + k, :, 128 * b : 128 * b + 128] = y[
                        size * b : size * b + size, 256 * s + 128 * k : 256 * s + 128 * k + 128
                    ]
    z = mm(x[3 * size :, :512], cvar[0])
    for s in range(SCALES):
        for k in range(3):
            for b in range(3):
                vari[s, k, :, 128 * b : 128 * b + 128] = z[
                    size * b : size * b + size, 384 * s + 128 * k : 384 * s + 128 * k + 128
                ]
    y = mm(xw[...], ctap[1])
    z = mm(xw[size:, :512], cvar[1])
    for s in range(SCALES):
        for k in range(2):
            here = slice(256 * s + 128 * k, 256 * s + 128 * k + 128)
            wave[s, k, :, 384:] = y[:size, here]
            wave[s, 2 + k, :, 384:] = y[size:, here]
        for k in range(3):
            vari[s, k, :, 384:] = z[:, 384 * s + 128 * k : 384 * s + 128 * k + 128]


def near_columns_kernel(total, wrap, ctap, cvar, wave, vari, token, x, xw):
    token[...] = jnp.zeros(token.shape, F32)

    def fields(f, j):
        if j < 4:
            return total[f, :, 128 * j : 128 * j + 128]
        return wrap[f, :, 128 * (j - 4) : 128 * (j - 3)]

    column_filters(HALF, fields, ctap, cvar, wave, vari, x, xw)


def far_columns_kernel(total, outer, inner, lat_rows, ctap, cvar, wave, vari, x, xw):
    _, core, _ = where_am_i()
    wrap = [seam(total[f], outer[f], unpack(inner[f]), core) for f in range(2)]

    def fields(f, j):
        if j < 4:
            mine = total[f, :, 128 * j : 128 * j + 128]
        else:
            mine = wrap[f][:, 128 * (j - 4) : 128 * (j - 3)]
        return jnp.concatenate([mine, lat_rows[f, :, 128 * j : 128 * j + 128]], axis=0)

    column_filters(HALF + RAD, fields, ctap, cvar, wave, vari, x, xw)


def final_kernel(
    near_wave, near_vari, far_wave, far_vari, sums, last,
    far_tap, near_tap, far_var, near_var, out, rate, fw, fv, nw, nv,
):
    _, core, lat = where_am_i()
    whole = sums[...] + last[...]
    own = whole[0:1] / whole[1:2]
    other = whole[2:3] / whole[3:4]
    table = tap_scales()

    def column(row):
        return jnp.transpose(jnp.broadcast_to(row, (128, 128)))

    lo, hi = own[:, :128], own[:, 128:]
    rate[0] = column(jnp.where(lat == 0, lo, hi))
    rate[1] = column(jnp.where(lat == 0, hi, lo))
    halo = column(jnp.where(lat == 0, other[:, :128], other[:, 128:]))
    rate[2, :RAD] = jnp.where(lat == 0, halo[:RAD], halo[96:])
    near_edge = pl.ds(pl.multiple_of(96 * lat, 32), RAD)
    far_edge = pl.ds(pl.multiple_of(96 * (1 - lat), 32), RAD)
    all_rows = slice(0, HALF)
    halo_rows = slice(HALF, HALF + RAD)
    far_parts = ((0, all_rows, 0, all_rows, 0), (1, near_edge, 1, near_edge, HALF))
    near_parts = (
        (1, all_rows, 1, all_rows, 0),
        (0, far_edge, 0, far_edge, HALF),
        (0, halo_rows, 2, slice(0, RAD), HALF + RAD),
    )
    waves = (far_wave, near_wave)
    varis = (far_vari, near_vari)

    def prepare(s):
        factor = [1.0 / (table[s][0] * table[s][2]), 1.0 / table[s][1] ** 2]
        factor.append(factor[0])
        slot = s
        for parts, span, w, v in ((far_parts, FAR_K, fw, fv), (near_parts, NEAR_K, nw, nv)):
            for source, rows, which, rrows, at in parts:
                size = HALF if at == 0 else RAD
                r = rate[which, rrows, :]
                for j in range(4):
                    cols = slice(128 * j, 128 * j + 128)
                    for k in range(2):
                        t = waves[source][s, k, rows, cols] - r * waves[source][s, 2 + k, rows, cols]
                        high, low = split(t)
                        for copy, t in ((0, high), (1, high), (2, low)):
                            first = span * (2 * copy + k) + at
                            w[slot, first : first + size, cols] = t
                    for k in range(3):
                        t = varis[source][s, k, rows, cols] * (r * factor[k])
                        for copy, t in enumerate(split(t)):
                            first = span * (3 * copy + k) + at
                            v[slot, first : first + size, cols] = t

    def multiply(s):
        slot = s
        for w, v, tap, var, start in (
            (fw, fv, far_tap, far_var, HALF * lat),
            (nw, nv, near_tap, near_var, HALF * (1 - lat)),
        ):
            wavelet = mm(tap[s], w[slot])
            variance = mm(var[s], v[slot])
            signal = wavelet * lax.rsqrt(jnp.maximum(variance, 1.0))
            there = pl.ds(pl.multiple_of(start, HALF), HALF)
            out[s, there, :] = pltpu.roll(signal, 64, 1)

    @pl.when(lat >= 0)
    def _():
        for s in range(SCALES):
            prepare(s)

    @pl.when(lat >= 0)
    def _():
        for s in range(SCALES):
            multiply(s)


VMEM = pl.BlockSpec(memory_space=pltpu.VMEM)
ANY = pl.BlockSpec(memory_space=pl.ANY)


def call(kernel, outs, ins, scratch=(), after=(), us=0.01, limit=36):
    count = len(ins)

    def body(*refs):
        kernel(*refs[:count], *refs[count + len(after) :])

    def run(*operands):
        return pl.pallas_call(
            body,
            out_shape=[jax.ShapeDtypeStruct(shape, dtype) for shape, dtype in outs],
            in_specs=list(ins) + [ANY] * len(after),
            out_specs=[VMEM] * len(outs),
            scratch_shapes=list(scratch),
            compiler_params=pltpu.CompilerParams(vmem_limit_bytes=limit * 1024 * 1024),
            cost_estimate=pl.CostEstimate(
                flops=0, bytes_accessed=int(us * 3.6e6), transcendentals=0
            ),
        )(*operands, *after)

    return run


TOKEN = (4, 2 * HALF)
TAPS = [
    ((2, 768, 256 * SCALES), BF16),
    ((2, 512, 384 * SCALES), BF16),
    ((SCALES, HALF, 6 * FAR_K), BF16),
    ((SCALES, HALF, 6 * NEAR_K), BF16),
    ((SCALES, HALF, 6 * FAR_K), BF16),
    ((SCALES, HALF, 6 * NEAR_K), BF16),
]
FINAL_SCRATCH = [pltpu.VMEM((3, HALF, 128), F32)] + [
    pltpu.VMEM((SCALES, 6 * span, TW), BF16) for span in (FAR_K, FAR_K, NEAR_K, NEAR_K)
]


def columns_scratch(rows):
    return [pltpu.VMEM((6 * rows, 768), BF16), pltpu.VMEM((2 * rows, 768), BF16)]


def columns_out(rows):
    return [((SCALES, 4, rows, TW), F32), ((SCALES, 3, rows, TW), F32)]


def per_device(counts_blocks, exposure_blocks, expo_col, expo_count):
    piece = (2, HALF, TW)
    blocks = (4, 2 * HALF, TW)

    def on_lon(value, step):
        return lax.ppermute(value, "lon", [(i, step(i) % LON) for i in range(LON)])

    def two_out(i):
        return i + 2 if i % 2 else i - 2

    def one_out(i):
        return i + 1 if i % 2 else i - 1

    def partner(i):
        return i ^ 1

    inputs = (expo_col, expo_count, counts_blocks, exposure_blocks)
    scalars = [pltpu.SMEM((4,), jnp.int32), pltpu.SMEM((1,), jnp.int32)]
    semaphores = [pltpu.SemaphoreType.DMA((2,)), pltpu.SemaphoreType.DMA((2, 4))]
    b1, sums = call(
        first_kernel,
        [((2, 2 * HALF, TW), F32), ((2, 2 * HALF), F32)],
        [ANY] * 4,
        [pltpu.VMEM((2, 2 * HALF, 128), F32)]
        + scalars
        + [pltpu.VMEM(blocks, jnp.int32), pltpu.VMEM(blocks, F32)]
        + semaphores,
        limit=58,
    )(*inputs)
    sums = sums + on_lon(sums, partner)
    rest = call(
        rest_kernel,
        [(piece, F32)] * 4 + [((2,) + piece, F32)] * 2 + [(TOKEN, F32)],
        [ANY, ANY, VMEM, VMEM],
        [pltpu.VMEM((16, 8, TW), F32)] + scalars + semaphores[:1],
        after=[sums],
        us=3.0,
        limit=24,
    )
    q1n, q1f, q0n, q0f, an, af, rest_token = rest(*inputs)
    an = on_lon(an, partner)
    af = on_lon(af, partner)
    other = lax.ppermute(sums, "lat", [(0, 1), (1, 0)])
    sums = jnp.concatenate([sums, other], axis=0) + rest_token
    b1 = on_lon(b1, two_out)
    steps = [sums]
    (b1_token,) = call(token_kernel, [(TOKEN, F32)], [ANY])(b1)
    sums = sums + on_lon(sums, lambda i: i ^ 16)
    steps.append(sums + b1_token)
    ctap, cvar, far_tap, near_tap, far_var, near_var, taps_token = call(
        taps_kernel, TAPS + [(TOKEN, F32)], [], after=[steps[1]], us=3.0
    )()
    sums = steps[1]
    for flip in (32, 64, 2):
        sums = sums + on_lon(sums, lambda i: i ^ flip)
        if flip == 64:
            sums = sums + taps_token
        steps.append(sums)

    def merge(first, after, *pieces):
        return call(
            functools.partial(merge_kernel, first),
            [(piece, F32), ((2, HALF + 8, TW), F32)],
            [VMEM] * 4,
            after=after,
        )(*pieces)

    def totals(after, *pieces):
        return call(
            total_kernel,
            [(piece, F32), ((2, HALF, 128), F32), ((2, 8, TW), F32)],
            [VMEM] * 3,
            after=after,
        )(*pieces)

    partial_n, sent_n = merge(0, [steps[1]], q1n, q0n, an, b1)
    b2_n = on_lon(sent_n, one_out)
    partial_f, sent_f = merge(HALF, [steps[1]], q1f, q0f, af, b1)
    b2_f = on_lon(sent_f, one_out)
    total_n, outer_n, inner_n = totals([steps[3]], partial_n, b2_n, sent_n)
    inner_n = on_lon(inner_n, partner)
    wrap_n, message = call(
        seam_kernel, [((2, HALF, 256), F32), ((2, RAD, TW + 256), F32)], [VMEM] * 3
    )(total_n, outer_n, inner_n)
    lat_rows = lax.ppermute(message, "lat", [(0, 1), (1, 0)])
    near_wave, near_vari, near_token = call(
        near_columns_kernel,
        columns_out(HALF) + [(TOKEN, F32)],
        [VMEM] * 4,
        columns_scratch(HALF),
        us=4.0,
    )(total_n, wrap_n, ctap, cvar)
    sums = sums + near_token
    sums = sums + on_lon(sums, lambda i: i ^ 4)
    last = on_lon(sums, lambda i: i ^ 8)
    total_f, outer_f, inner_f = totals([steps[4]], partial_f, b2_f, sent_f)
    inner_f = on_lon(inner_f, partner)
    far_wave, far_vari = call(
        far_columns_kernel,
        columns_out(HALF + RAD),
        [VMEM] * 6,
        columns_scratch(HALF + RAD),
        us=5.0,
    )(total_f, outer_f, inner_f, lat_rows, ctap, cvar)
    (out,) = call(
        final_kernel, [((SCALES, 2 * HALF, TW), F32)], [VMEM] * 10, FINAL_SCRATCH
    )(near_wave, near_vari, far_wave, far_vari, sums, last, far_tap, near_tap, far_var, near_var)
    return out


def solution(mesh):
    placed = (P("lon", "lat", None), P("lon", "lat", None), P("lon"), P("lon"))
    return jax.shard_map(
        per_device, mesh=mesh, in_specs=placed, out_specs=P(None, "lat", "lon"), check_vma=False
    )
```

```python
import functools

import jax
import jax.numpy as jnp
import ml_dtypes
import numpy as np
from jax import lax
from jax.experimental import pallas as pl
from jax.experimental.pallas import tpu as pltpu
from jax.sharding import PartitionSpec as P

TW = 512
RAD = 32
SCALES = 3
LON = 128
HALF = 128
FAR_K = 160
NEAR_K = 192
F32 = jnp.float32
BF16 = jnp.bfloat16


def iota(shape, dim):
    return lax.broadcasted_iota(jnp.int32, shape, dim)


def where_am_i():
    lon = lax.axis_index("lon")
    return lon, lax.rem(lon, 2), lax.axis_index("lat")


def pack(x):
    lane = iota((8, 128), 1)
    parts = []
    for j in range(4):
        a = x[32 * j : 32 * j + 8]
        for m in range(1, 4):
            b = pltpu.roll(x[32 * j + 8 * m : 32 * j + 8 * m + 8], 32 * m, 1)
            a = jnp.where(lane < 32 * m, a, b)
        parts.append(a)
    return jnp.concatenate(parts, axis=1)


def unpack(p):
    parts = []
    for j in range(4):
        v = p[:, 128 * j : 128 * j + 128]
        parts.append(v)
        for m in range(1, 4):
            parts.append(pltpu.roll(v, 128 - 32 * m, 1))
    return jnp.concatenate(parts, axis=0)


def slot_place(cols, slot, lon):
    column = cols[slot]
    first = column // TW
    within = column - first * TW
    rel = lax.rem(first - lon + LON + LON // 2, LON) - LON // 2
    return within, rel


def fetch_scalars(cols_hbm, count_hbm, cols, count, sem):
    copies = [
        pltpu.make_async_copy(cols_hbm, cols, sem.at[0]),
        pltpu.make_async_copy(count_hbm, count, sem.at[1]),
    ]
    for copy in copies:
        copy.start()
    return copies


def first_kernel(
    cols_hbm, count_hbm, c_hbm, e_hbm, out, sums, acc, cols, count, cbuf, ebuf, ssem, sem
):
    lon, core, lat = where_am_i()
    scalars = fetch_scalars(cols_hbm, count_hbm, cols, count, ssem)
    copies = []
    for slot in range(4):
        copies.append(pltpu.make_async_copy(c_hbm.at[slot], cbuf.at[slot], sem.at[0, slot]))
        copies.append(pltpu.make_async_copy(e_hbm.at[slot], ebuf.at[slot], sem.at[1, slot]))
    for copy in copies:
        copy.start()
    wanted = jnp.where(core == 1, 1, -2)
    out[...] = jnp.zeros(out.shape, F32)
    acc[...] = jnp.zeros(acc.shape, F32)
    for copy in scalars:
        copy.wait()
    for slot in range(4):
        copies[2 * slot].wait()
        copies[2 * slot + 1].wait()

        @pl.when(slot < count[0])
        def _(slot=slot):
            def body(g, carry):
                rows = pl.ds(pl.multiple_of(8 * g, 8), 8)
                for f, buf in ((0, cbuf), (1, ebuf)):
                    x = buf[slot, rows, :].astype(F32)
                    x = (x[:, :128] + x[:, 128:256]) + (x[:, 256:384] + x[:, 384:])
                    acc[f, rows, :] += x
                return carry

            lax.fori_loop(0, 2 * HALF // 8, body, 0, unroll=8)

        within, rel = slot_place(cols, slot, lon)

        @pl.when(jnp.logical_and(slot < count[0], rel == wanted))
        def _(slot=slot, within=within):
            lane = iota((8, 128), 1)

            for first, start in ((0, HALF * (1 - lat)), (HALF, HALF * lat)):

                def body(g, carry, first=first, start=start):
                    rows = pl.ds(pl.multiple_of(start + 8 * g, 8), 8)
                    here = pl.ds(pl.multiple_of(first + 8 * g, 8), 8)
                    for f, buf in ((0, cbuf), (1, ebuf)):
                        x = rolled(buf, slot, rows, within)
                        for j in range(4):
                            col = lane + 128 * j
                            keep = jnp.where(core == 1, col - within, within - 1 - col) < 0
                            out[f, here, 128 * j : 128 * j + 128] += jnp.where(keep, x[j], 0.0)
                    return carry

                lax.fori_loop(0, HALF // 8, body, 0, unroll=4)

    for f in range(2):
        for j in range(2):
            block = jnp.transpose(acc[f, 128 * j : 128 * j + 128, :])
            sums[f : f + 1, 128 * j : 128 * j + 128] = jnp.sum(block, axis=0, keepdims=True)


def rolled(buf, slot, rows, within):
    whole = within // 128
    rest = within - 128 * whole
    first = iota((8, 128), 1) < rest
    turned = []
    for j in range(4):
        block = lax.rem(j + 4 - whole, 4)
        x = buf[slot, rows, pl.ds(pl.multiple_of(128 * block, 128), 128)].astype(F32)
        turned.append(pltpu.roll(x, rest, 1))
    return [jnp.where(first, turned[j - 1], turned[j]) for j in range(4)]


def rest_kernel(
    cols_hbm, count_hbm, cbuf, ebuf, q1n, q1f, q0n, q0f, an, af, token, weight, cols, count, ssem
):
    lon, core, lat = where_am_i()
    for copy in fetch_scalars(cols_hbm, count_hbm, cols, count, ssem):
        copy.wait()
    token[...] = jnp.zeros(token.shape, F32)
    sign = 2 * core - 1
    col = iota((8, TW), 1)
    shifts = []
    for slot in range(4):
        within, rel = slot_place(cols, slot, lon)
        alive = slot < count[0]
        shifts.append(within)
        for k, q in enumerate((1, 0, -1, -2)):
            high = jnp.where(jnp.logical_and(alive, rel * sign == q), 1.0, 0.0).astype(F32)
            low = jnp.where(jnp.logical_and(alive, (rel + 1) * sign == q), 1.0, 0.0).astype(F32)
            weight[4 * slot + k] = jnp.where(col >= within, high, low)
    for q1, q0, a, start in ((q1n, q0n, an, HALF * (1 - lat)), (q1f, q0f, af, HALF * lat)):

        def body(g, carry, q1=q1, q0=q0, a=a, start=start):
            rows = pl.ds(pl.multiple_of(start + 8 * g, 8), 8)
            here = pl.ds(pl.multiple_of(8 * g, 8), 8)
            for f, buf in ((0, cbuf), (1, ebuf)):
                xs = [rolled(buf, slot, rows, shifts[slot]) for slot in range(4)]
                for j in range(4):
                    block = slice(128 * j, 128 * j + 128)
                    outs = (q1.at[f], q0.at[f], a.at[0, f], a.at[1, f])
                    for k, out in enumerate(outs):
                        t = xs[0][j] * weight[k, :, block]
                        for slot in range(1, 4):
                            t = t + xs[slot][j] * weight[4 * slot + k, :, block]
                        out[here, block] = t
            return carry

        lax.fori_loop(0, HALF // 8, body, 0, unroll=4)


def token_kernel(arrived, token):
    token[...] = jnp.zeros(token.shape, F32)


def merge_kernel(first, q1, q0, a, b1, partial, message):
    _, core, _ = where_am_i()
    for f in range(2):
        message[f, :HALF, :] = q1[f] + a[1, f]
        mine = q0[f] + a[0, f] + b1[f, first : first + HALF, :]
        partial[f] = mine
        edge = jnp.where(core == 1, pltpu.roll(mine[:, 384:], 32, 1), mine[:, :128])
        message[f, HALF:, :] = pack(edge)


def total_kernel(partial, received, sent, total, outer, inner):
    _, core, _ = where_am_i()
    for f in range(2):
        mine = partial[f] + received[f, :HALF, :]
        total[f] = mine
        near = jnp.where(
            core == 1, sent[f, :HALF, :128], pltpu.roll(sent[f, :HALF, 384:], 32, 1)
        )
        outer[f] = unpack(received[f, HALF:, :]) + near
        edge = jnp.where(core == 1, mine[:, :128], pltpu.roll(mine[:, 384:], 32, 1))
        inner[f] = pack(edge)


def seam(total, outer, inner, core):
    lane = iota((HALF, 128), 1)
    left = jnp.where(core == 1, inner, outer)
    right = jnp.where(core == 1, outer, inner)
    a = jnp.where(lane < 96, pltpu.roll(total[:, 384:], 96, 1), pltpu.roll(right, 96, 1))
    b = jnp.where(lane < 32, left, pltpu.roll(total[:, :128], 32, 1))
    return jnp.concatenate([a, b], axis=1)


def seam_kernel(total, outer, inner, wrap, message):
    _, core, lat = where_am_i()
    rows = pl.ds(pl.multiple_of(96 * (1 - lat), 32), 32)
    for f in range(2):
        wrap[f] = seam(total[f], outer[f], unpack(inner[f]), core)
        message[f, :, :TW] = total[f, rows, :]
        message[f, :, TW:] = wrap[f, rows, :]


def bell_hat(offset, sigma):
    inside = jnp.abs(offset) <= RAD
    d = offset.astype(F32)
    bell = jnp.where(inside, jnp.exp(-d * d / (2.0 * sigma * sigma)), 0.0)
    hat = (1.0 - d * d / (sigma * sigma)) * bell
    return bell, hat


def split(x):
    high = x.astype(BF16)
    return high, (x - high.astype(F32)).astype(BF16)


@functools.cache
def tap_scales():
    t = np.arange(-RAD, RAD + 1, dtype=np.float64)
    table = []
    for s in range(SCALES):
        sigma = RAD / 2.0 ** (4 - s)
        g = np.exp(-t * t / (2.0 * sigma * sigma))
        h = (1.0 - t * t / (sigma * sigma)) * g
        row = []
        for k in (h * h, h * g, g * g):
            c = 1.0 + np.arange(4096) / 4096.0
            error = (k * c[:, None]).astype(ml_dtypes.bfloat16).astype(np.float64) / c[:, None] - k
            cost = np.abs(error.sum(1)) / np.abs(k).sum()
            cost = 4.0 * cost + np.sqrt((error**2).sum(1) / (k**2).sum())
            row.append(float(c[np.argmin(cost)]))
        table.append(row)
    return table


def taps_kernel(ctap, cvar, far_tap, near_tap, far_var, near_var, token):
    _, _, lat = where_am_i()
    token[...] = jnp.zeros(token.shape, F32)
    w = iota((256, 128), 0)
    n = iota((256, 128), 1)
    straight = w - n - 64
    wrapped_w = jnp.where(w < 128, 416 + w, w - 160)
    wrapped_n = jnp.where(n < 64, 448 + n, n - 64)
    a = iota((HALF, 128), 0)
    b = iota((HALF, 128), 1)
    table = tap_scales()

    def far_row(p):
        return jnp.where(lat == 0, p, jnp.where(p < HALF, p + HALF, p - 32))

    def near_row(p):
        inner = jnp.where(lat == 0, p + HALF, p)
        adjacent = jnp.where(lat == 0, p - 32, p)
        halo = jnp.where(lat == 0, p + 96, p - 192)
        return jnp.where(p < HALF, inner, jnp.where(p < HALF + 32, adjacent, halo))

    for s in range(SCALES):
        sigma = RAD / 2.0 ** (4 - s)
        chh, chg, cgg = table[s]
        for kind, offset in ((0, straight), (1, wrapped_w - wrapped_n)):
            bell, hat = bell_hat(offset, sigma)
            for k, t in enumerate((hat, bell)):
                high, low = split(t)
                here = slice(256 * s + 128 * k, 256 * s + 128 * k + 128)
                ctap[kind, :256, here] = high
                ctap[kind, 256:512, here] = high
                ctap[kind, 512:, here] = low
            for k, t in enumerate((chh * hat * hat, chg * hat * bell, cgg * bell * bell)):
                here = slice(384 * s + 128 * k, 384 * s + 128 * k + 128)
                t = t.astype(BF16)
                cvar[kind, :256, here] = t
                cvar[kind, 256:, here] = t
        for tap, var, span, place in (
            (far_tap, far_var, FAR_K, far_row),
            (near_tap, near_var, NEAR_K, near_row),
        ):
            for j in range(-(-6 * span // 128)):
                here = slice(128 * j, min(128 * j + 128, 6 * span))
                size = here.stop - here.start
                lane = 128 * j + b
                copy = (lane >= 2 * span).astype(jnp.int32) + (lane >= 4 * span).astype(jnp.int32)
                p = lane - 2 * span * copy
                second = p >= span
                bell, hat = bell_hat(place(jnp.where(second, p - span, p)) - place(a), sigma)
                high, low = split(jnp.where(second, hat, bell))
                t = jnp.where(copy == 1, low.astype(F32), high.astype(F32)).astype(BF16)
                tap[s, :, here] = t[:, :size]
                p = jnp.where(lane >= 3 * span, lane - 3 * span, lane)
                which = (p >= span).astype(jnp.int32) + (p >= 2 * span).astype(jnp.int32)
                bell, hat = bell_hat(place(p - span * which) - place(a), sigma)
                t = jnp.where(which == 1, (2.0 * chg) * hat * bell, chh * hat * hat)
                t = jnp.where(which == 0, cgg * bell * bell, t).astype(BF16)
                var[s, :, here] = t[:, :size]


def mm(a, b):
    return jnp.dot(a, b, preferred_element_type=F32)


def column_filters(size, fields, ctap, cvar, wave, vari, x, xw):
    for j in range(6):
        for f in range(2):
            high, low = split(fields(f, j))
            if j < 4:
                places = [(x, 3 * f + b, j - b) for b in range(3) if j - b in (0, 1)]
            else:
                places = [(xw, f, j - 4)]
            for ref, b, side in places:
                rows = slice(size * b, size * b + size)
                ref[rows, 128 * side : 128 * side + 128] = high
                ref[rows, 256 + 128 * side : 384 + 128 * side] = low
                ref[rows, 512 + 128 * side : 640 + 128 * side] = high
    for f in range(2):
        y = mm(x[3 * size * f : 3 * size * (f + 1), :], ctap[0])
        for s in range(SCALES):
            for k in range(2):
                for b in range(3):
                    wave[s, 2 * f + k, :, 128 * b : 128 * b + 128] = y[
                        size * b : size * b + size, 256 * s + 128 * k : 256 * s + 128 * k + 128
                    ]
    z = mm(x[3 * size :, :512], cvar[0])
    for s in range(SCALES):
        for k in range(3):
            for b in range(3):
                vari[s, k, :, 128 * b : 128 * b + 128] = z[
                    size * b : size * b + size, 384 * s + 128 * k : 384 * s + 128 * k + 128
                ]
    y = mm(xw[...], ctap[1])
    z = mm(xw[size:, :512], cvar[1])
    for s in range(SCALES):
        for k in range(2):
            here = slice(256 * s + 128 * k, 256 * s + 128 * k + 128)
            wave[s, k, :, 384:] = y[:size, here]
            wave[s, 2 + k, :, 384:] = y[size:, here]
        for k in range(3):
            vari[s, k, :, 384:] = z[:, 384 * s + 128 * k : 384 * s + 128 * k + 128]


def near_columns_kernel(total, wrap, ctap, cvar, wave, vari, token, x, xw):
    token[...] = jnp.zeros(token.shape, F32)

    def fields(f, j):
        if j < 4:
            return total[f, :, 128 * j : 128 * j + 128]
        return wrap[f, :, 128 * (j - 4) : 128 * (j - 3)]

    column_filters(HALF, fields, ctap, cvar, wave, vari, x, xw)


def far_columns_kernel(total, outer, inner, lat_rows, ctap, cvar, wave, vari, x, xw):
    _, core, _ = where_am_i()
    wrap = [seam(total[f], outer[f], unpack(inner[f]), core) for f in range(2)]

    def fields(f, j):
        if j < 4:
            mine = total[f, :, 128 * j : 128 * j + 128]
        else:
            mine = wrap[f][:, 128 * (j - 4) : 128 * (j - 3)]
        return jnp.concatenate([mine, lat_rows[f, :, 128 * j : 128 * j + 128]], axis=0)

    column_filters(HALF + RAD, fields, ctap, cvar, wave, vari, x, xw)


def final_kernel(
    near_wave, near_vari, far_wave, far_vari, sums, last,
    far_tap, near_tap, far_var, near_var, out, rate, fw, fv, nw, nv,
):
    _, core, lat = where_am_i()
    whole = sums[...] + last[...]
    own = whole[0:1] / whole[1:2]
    other = whole[2:3] / whole[3:4]
    table = tap_scales()

    def column(row):
        return jnp.transpose(jnp.broadcast_to(row, (128, 128)))

    lo, hi = own[:, :128], own[:, 128:]
    rate[0] = column(jnp.where(lat == 0, lo, hi))
    rate[1] = column(jnp.where(lat == 0, hi, lo))
    halo = column(jnp.where(lat == 0, other[:, :128], other[:, 128:]))
    rate[2, :RAD] = jnp.where(lat == 0, halo[:RAD], halo[96:])
    near_edge = pl.ds(pl.multiple_of(96 * lat, 32), RAD)
    far_edge = pl.ds(pl.multiple_of(96 * (1 - lat), 32), RAD)
    all_rows = slice(0, HALF)
    halo_rows = slice(HALF, HALF + RAD)
    far_parts = ((0, all_rows, 0, all_rows, 0), (1, near_edge, 1, near_edge, HALF))
    near_parts = (
        (1, all_rows, 1, all_rows, 0),
        (0, far_edge, 0, far_edge, HALF),
        (0, halo_rows, 2, slice(0, RAD), HALF + RAD),
    )
    waves = (far_wave, near_wave)
    varis = (far_vari, near_vari)

    def prepare(s):
        factor = [1.0 / (table[s][0] * table[s][2]), 1.0 / table[s][1] ** 2]
        factor.append(factor[0])
        slot = s
        for parts, span, w, v in ((far_parts, FAR_K, fw, fv), (near_parts, NEAR_K, nw, nv)):
            for source, rows, which, rrows, at in parts:
                size = HALF if at == 0 else RAD
                r = rate[which, rrows, :]
                for j in range(4):
                    cols = slice(128 * j, 128 * j + 128)
                    for k in range(2):
                        t = waves[source][s, k, rows, cols] - r * waves[source][s, 2 + k, rows, cols]
                        high, low = split(t)
                        for copy, t in ((0, high), (1, high), (2, low)):
                            first = span * (2 * copy + k) + at
                            w[slot, first : first + size, cols] = t
                    for k in range(3):
                        t = varis[source][s, k, rows, cols] * (r * factor[k])
                        for copy, t in enumerate(split(t)):
                            first = span * (3 * copy + k) + at
                            v[slot, first : first + size, cols] = t

    def multiply(s):
        slot = s
        for w, v, tap, var, start in (
            (fw, fv, far_tap, far_var, HALF * lat),
            (nw, nv, near_tap, near_var, HALF * (1 - lat)),
        ):
            wavelet = mm(tap[s], w[slot])
            variance = mm(var[s], v[slot])
            signal = wavelet * lax.rsqrt(jnp.maximum(variance, 1.0))
            there = pl.ds(pl.multiple_of(start, HALF), HALF)
            out[s, there, :] = pltpu.roll(signal, 64, 1)

    @pl.when(lat >= 0)
    def _():
        for s in range(SCALES):
            prepare(s)

    @pl.when(lat >= 0)
    def _():
        for s in range(SCALES):
            multiply(s)


VMEM = pl.BlockSpec(memory_space=pltpu.VMEM)
ANY = pl.BlockSpec(memory_space=pl.ANY)


def call(kernel, outs, ins, scratch=(), after=(), us=0.01, limit=36):
    count = len(ins)

    def body(*refs):
        kernel(*refs[:count], *refs[count + len(after) :])

    def run(*operands):
        return pl.pallas_call(
            body,
            out_shape=[jax.ShapeDtypeStruct(shape, dtype) for shape, dtype in outs],
            in_specs=list(ins) + [ANY] * len(after),
            out_specs=[VMEM] * len(outs),
            scratch_shapes=list(scratch),
            compiler_params=pltpu.CompilerParams(vmem_limit_bytes=limit * 1024 * 1024),
            cost_estimate=pl.CostEstimate(
                flops=0, bytes_accessed=int(us * 3.6e6), transcendentals=0
            ),
        )(*operands, *after)

    return run


TOKEN = (4, 2 * HALF)
TAPS = [
    ((2, 768, 256 * SCALES), BF16),
    ((2, 512, 384 * SCALES), BF16),
    ((SCALES, HALF, 6 * FAR_K), BF16),
    ((SCALES, HALF, 6 * NEAR_K), BF16),
    ((SCALES, HALF, 6 * FAR_K), BF16),
    ((SCALES, HALF, 6 * NEAR_K), BF16),
]
FINAL_SCRATCH = [pltpu.VMEM((3, HALF, 128), F32)] + [
    pltpu.VMEM((SCALES, 6 * span, TW), BF16) for span in (FAR_K, FAR_K, NEAR_K, NEAR_K)
]


def columns_scratch(rows):
    return [pltpu.VMEM((6 * rows, 768), BF16), pltpu.VMEM((2 * rows, 768), BF16)]


def columns_out(rows):
    return [((SCALES, 4, rows, TW), F32), ((SCALES, 3, rows, TW), F32)]


def per_device(counts_blocks, exposure_blocks, expo_col, expo_count):
    piece = (2, HALF, TW)
    blocks = (4, 2 * HALF, TW)

    def on_lon(value, step):
        return lax.ppermute(value, "lon", [(i, step(i) % LON) for i in range(LON)])

    def two_out(i):
        return i + 2 if i % 2 else i - 2

    def one_out(i):
        return i + 1 if i % 2 else i - 1

    def partner(i):
        return i ^ 1

    inputs = (expo_col, expo_count, counts_blocks, exposure_blocks)
    scalars = [pltpu.SMEM((4,), jnp.int32), pltpu.SMEM((1,), jnp.int32)]
    semaphores = [pltpu.SemaphoreType.DMA((2,)), pltpu.SemaphoreType.DMA((2, 4))]
    b1, sums = call(
        first_kernel,
        [((2, 2 * HALF, TW), F32), ((2, 2 * HALF), F32)],
        [ANY] * 4,
        [pltpu.VMEM((2, 2 * HALF, 128), F32)]
        + scalars
        + [pltpu.VMEM(blocks, jnp.int32), pltpu.VMEM(blocks, F32)]
        + semaphores,
        limit=58,
    )(*inputs)
    sums = sums + on_lon(sums, partner)
    rest = call(
        rest_kernel,
        [(piece, F32)] * 4 + [((2,) + piece, F32)] * 2 + [(TOKEN, F32)],
        [ANY, ANY, VMEM, VMEM],
        [pltpu.VMEM((16, 8, TW), F32)] + scalars + semaphores[:1],
        after=[sums],
        us=1.0,
        limit=24,
    )
    q1n, q1f, q0n, q0f, an, af, rest_token = rest(*inputs)
    an = on_lon(an, partner)
    af = on_lon(af, partner)
    other = lax.ppermute(sums, "lat", [(0, 1), (1, 0)])
    sums = jnp.concatenate([sums, other], axis=0) + rest_token
    b1 = on_lon(b1, two_out)
    steps = [sums]
    (b1_token,) = call(token_kernel, [(TOKEN, F32)], [ANY])(b1)
    sums = sums + on_lon(sums, lambda i: i ^ 16)
    steps.append(sums + b1_token)
    ctap, cvar, far_tap, near_tap, far_var, near_var, taps_token = call(
        taps_kernel, TAPS + [(TOKEN, F32)], [], after=[steps[1]], us=3.0
    )()
    sums = steps[1]
    for flip in (32, 64, 2):
        sums = sums + on_lon(sums, lambda i: i ^ flip)
        if flip == 64:
            sums = sums + taps_token
        steps.append(sums)

    def merge(first, after, *pieces):
        return call(
            functools.partial(merge_kernel, first),
            [(piece, F32), ((2, HALF + 8, TW), F32)],
            [VMEM] * 4,
            after=after,
        )(*pieces)

    def totals(after, *pieces):
        return call(
            total_kernel,
            [(piece, F32), ((2, HALF, 128), F32), ((2, 8, TW), F32)],
            [VMEM] * 3,
            after=after,
        )(*pieces)

    partial_n, sent_n = merge(0, [steps[1]], q1n, q0n, an, b1)
    b2_n = on_lon(sent_n, one_out)
    partial_f, sent_f = merge(HALF, [steps[1]], q1f, q0f, af, b1)
    b2_f = on_lon(sent_f, one_out)
    total_n, outer_n, inner_n = totals([steps[2]], partial_n, b2_n, sent_n)
    inner_n = on_lon(inner_n, partner)
    wrap_n, message = call(
        seam_kernel, [((2, HALF, 256), F32), ((2, RAD, TW + 256), F32)], [VMEM] * 3
    )(total_n, outer_n, inner_n)
    lat_rows = lax.ppermute(message, "lat", [(0, 1), (1, 0)])
    near_wave, near_vari, near_token = call(
        near_columns_kernel,
        columns_out(HALF) + [(TOKEN, F32)],
        [VMEM] * 4,
        columns_scratch(HALF),
        us=4.0,
    )(total_n, wrap_n, ctap, cvar)
    sums = sums + near_token
    sums = sums + on_lon(sums, lambda i: i ^ 4)
    last = on_lon(sums, lambda i: i ^ 8)
    total_f, outer_f, inner_f = totals([steps[4]], partial_f, b2_f, sent_f)
    inner_f = on_lon(inner_f, partner)
    far_wave, far_vari = call(
        far_columns_kernel,
        columns_out(HALF + RAD),
        [VMEM] * 6,
        columns_scratch(HALF + RAD),
        us=5.0,
    )(total_f, outer_f, inner_f, lat_rows, ctap, cvar)
    (out,) = call(
        final_kernel, [((SCALES, 2 * HALF, TW), F32)], [VMEM] * 10, FINAL_SCRATCH
    )(near_wave, near_vari, far_wave, far_vari, sums, last, far_tap, near_tap, far_var, near_var)
    return out


def solution(mesh):
    placed = (P("lon", "lat", None), P("lon", "lat", None), P("lon"), P("lon"))
    return jax.shard_map(
        per_device, mesh=mesh, in_specs=placed, out_specs=P(None, "lat", "lon"), check_vma=False
    )
```

```python
import functools

import jax
import jax.numpy as jnp
import ml_dtypes
import numpy as np
from jax import lax
from jax.experimental import pallas as pl
from jax.experimental.pallas import tpu as pltpu
from jax.sharding import PartitionSpec as P

TW = 512
RAD = 32
SCALES = 3
LON = 128
HALF = 128
FAR_K = 160
NEAR_K = 192
F32 = jnp.float32
BF16 = jnp.bfloat16


def iota(shape, dim):
    return lax.broadcasted_iota(jnp.int32, shape, dim)


def where_am_i():
    lon = lax.axis_index("lon")
    return lon, lax.rem(lon, 2), lax.axis_index("lat")


def pack(x):
    lane = iota((8, 128), 1)
    parts = []
    for j in range(4):
        a = x[32 * j : 32 * j + 8]
        for m in range(1, 4):
            b = pltpu.roll(x[32 * j + 8 * m : 32 * j + 8 * m + 8], 32 * m, 1)
            a = jnp.where(lane < 32 * m, a, b)
        parts.append(a)
    return jnp.concatenate(parts, axis=1)


def unpack(p):
    parts = []
    for j in range(4):
        v = p[:, 128 * j : 128 * j + 128]
        parts.append(v)
        for m in range(1, 4):
            parts.append(pltpu.roll(v, 128 - 32 * m, 1))
    return jnp.concatenate(parts, axis=0)


def slot_place(cols, slot, lon):
    column = cols[slot]
    first = column // TW
    within = column - first * TW
    rel = lax.rem(first - lon + LON + LON // 2, LON) - LON // 2
    return within, rel


def fetch_scalars(cols_hbm, count_hbm, cols, count, sem):
    copies = [
        pltpu.make_async_copy(cols_hbm, cols, sem.at[0]),
        pltpu.make_async_copy(count_hbm, count, sem.at[1]),
    ]
    for copy in copies:
        copy.start()
    return copies


def first_kernel(
    cols_hbm, count_hbm, c_hbm, e_hbm, out, sums, acc, cols, count, cbuf, ebuf, ssem, sem
):
    lon, core, lat = where_am_i()
    scalars = fetch_scalars(cols_hbm, count_hbm, cols, count, ssem)
    copies = []
    for slot in range(4):
        copies.append(pltpu.make_async_copy(c_hbm.at[slot], cbuf.at[slot], sem.at[0, slot]))
        copies.append(pltpu.make_async_copy(e_hbm.at[slot], ebuf.at[slot], sem.at[1, slot]))
    for copy in copies:
        copy.start()
    wanted = jnp.where(core == 1, 1, -2)
    out[...] = jnp.zeros(out.shape, F32)
    acc[...] = jnp.zeros(acc.shape, F32)
    for copy in scalars:
        copy.wait()
    for slot in range(4):
        copies[2 * slot].wait()
        copies[2 * slot + 1].wait()

        @pl.when(slot < count[0])
        def _(slot=slot):
            def body(g, carry):
                rows = pl.ds(pl.multiple_of(8 * g, 8), 8)
                for f, buf in ((0, cbuf), (1, ebuf)):
                    x = buf[slot, rows, :].astype(F32)
                    x = (x[:, :128] + x[:, 128:256]) + (x[:, 256:384] + x[:, 384:])
                    acc[f, rows, :] += x
                return carry

            lax.fori_loop(0, 2 * HALF // 8, body, 0, unroll=8)

        within, rel = slot_place(cols, slot, lon)

        @pl.when(jnp.logical_and(slot < count[0], rel == wanted))
        def _(slot=slot, within=within):
            lane = iota((8, 128), 1)

            for first, start in ((0, HALF * (1 - lat)), (HALF, HALF * lat)):

                def body(g, carry, first=first, start=start):
                    rows = pl.ds(pl.multiple_of(start + 8 * g, 8), 8)
                    here = pl.ds(pl.multiple_of(first + 8 * g, 8), 8)
                    for f, buf in ((0, cbuf), (1, ebuf)):
                        x = rolled(buf, slot, rows, within)
                        for j in range(4):
                            col = lane + 128 * j
                            keep = jnp.where(core == 1, col - within, within - 1 - col) < 0
                            out[f, here, 128 * j : 128 * j + 128] += jnp.where(keep, x[j], 0.0)
                    return carry

                lax.fori_loop(0, HALF // 8, body, 0, unroll=4)

    for f in range(2):
        for j in range(2):
            block = jnp.transpose(acc[f, 128 * j : 128 * j + 128, :])
            sums[f : f + 1, 128 * j : 128 * j + 128] = jnp.sum(block, axis=0, keepdims=True)


def rolled(buf, slot, rows, within):
    whole = within // 128
    rest = within - 128 * whole
    first = iota((8, 128), 1) < rest
    turned = []
    for j in range(4):
        block = lax.rem(j + 4 - whole, 4)
        x = buf[slot, rows, pl.ds(pl.multiple_of(128 * block, 128), 128)].astype(F32)
        turned.append(pltpu.roll(x, rest, 1))
    return [jnp.where(first, turned[j - 1], turned[j]) for j in range(4)]


def rest_kernel(
    cols_hbm, count_hbm, cbuf, ebuf, q1n, q1f, q0n, q0f, an, af, token, weight, cols, count, ssem
):
    lon, core, lat = where_am_i()
    for copy in fetch_scalars(cols_hbm, count_hbm, cols, count, ssem):
        copy.wait()
    token[...] = jnp.zeros(token.shape, F32)
    sign = 2 * core - 1
    col = iota((8, TW), 1)
    shifts = []
    for slot in range(4):
        within, rel = slot_place(cols, slot, lon)
        alive = slot < count[0]
        shifts.append(within)
        for k, q in enumerate((1, 0, -1, -2)):
            high = jnp.where(jnp.logical_and(alive, rel * sign == q), 1.0, 0.0).astype(F32)
            low = jnp.where(jnp.logical_and(alive, (rel + 1) * sign == q), 1.0, 0.0).astype(F32)
            weight[4 * slot + k] = jnp.where(col >= within, high, low)
    for q1, q0, a, start in ((q1n, q0n, an, HALF * (1 - lat)), (q1f, q0f, af, HALF * lat)):

        def body(g, carry, q1=q1, q0=q0, a=a, start=start):
            rows = pl.ds(pl.multiple_of(start + 8 * g, 8), 8)
            here = pl.ds(pl.multiple_of(8 * g, 8), 8)
            for f, buf in ((0, cbuf), (1, ebuf)):
                xs = [rolled(buf, slot, rows, shifts[slot]) for slot in range(4)]
                for j in range(4):
                    block = slice(128 * j, 128 * j + 128)
                    outs = (q1.at[f], q0.at[f], a.at[0, f], a.at[1, f])
                    for k, out in enumerate(outs):
                        t = xs[0][j] * weight[k, :, block]
                        for slot in range(1, 4):
                            t = t + xs[slot][j] * weight[4 * slot + k, :, block]
                        out[here, block] = t
            return carry

        lax.fori_loop(0, HALF // 8, body, 0, unroll=4)


def token_kernel(arrived, token):
    token[...] = jnp.zeros(token.shape, F32)


def merge_kernel(first, q1, q0, a, b1, partial, message):
    _, core, _ = where_am_i()
    for f in range(2):
        message[f, :HALF, :] = q1[f] + a[1, f]
        mine = q0[f] + a[0, f] + b1[f, first : first + HALF, :]
        partial[f] = mine
        edge = jnp.where(core == 1, pltpu.roll(mine[:, 384:], 32, 1), mine[:, :128])
        message[f, HALF:, :] = pack(edge)


def total_kernel(partial, received, sent, total, outer, inner):
    _, core, _ = where_am_i()
    for f in range(2):
        mine = partial[f] + received[f, :HALF, :]
        total[f] = mine
        near = jnp.where(
            core == 1, sent[f, :HALF, :128], pltpu.roll(sent[f, :HALF, 384:], 32, 1)
        )
        outer[f] = unpack(received[f, HALF:, :]) + near
        edge = jnp.where(core == 1, mine[:, :128], pltpu.roll(mine[:, 384:], 32, 1))
        inner[f] = pack(edge)


def seam(total, outer, inner, core):
    lane = iota((HALF, 128), 1)
    left = jnp.where(core == 1, inner, outer)
    right = jnp.where(core == 1, outer, inner)
    a = jnp.where(lane < 96, pltpu.roll(total[:, 384:], 96, 1), pltpu.roll(right, 96, 1))
    b = jnp.where(lane < 32, left, pltpu.roll(total[:, :128], 32, 1))
    return jnp.concatenate([a, b], axis=1)


def seam_kernel(total, outer, inner, wrap, message):
    _, core, lat = where_am_i()
    rows = pl.ds(pl.multiple_of(96 * (1 - lat), 32), 32)
    for f in range(2):
        wrap[f] = seam(total[f], outer[f], unpack(inner[f]), core)
        message[f, :, :TW] = total[f, rows, :]
        message[f, :, TW:] = wrap[f, rows, :]


def bell_hat(offset, sigma):
    inside = jnp.abs(offset) <= RAD
    d = offset.astype(F32)
    bell = jnp.where(inside, jnp.exp(-d * d / (2.0 * sigma * sigma)), 0.0)
    hat = (1.0 - d * d / (sigma * sigma)) * bell
    return bell, hat


def split(x):
    high = x.astype(BF16)
    return high, (x - high.astype(F32)).astype(BF16)


@functools.cache
def tap_scales():
    t = np.arange(-RAD, RAD + 1, dtype=np.float64)
    table = []
    for s in range(SCALES):
        sigma = RAD / 2.0 ** (4 - s)
        g = np.exp(-t * t / (2.0 * sigma * sigma))
        h = (1.0 - t * t / (sigma * sigma)) * g
        row = []
        for k in (h * h, h * g, g * g):
            c = 1.0 + np.arange(4096) / 4096.0
            error = (k * c[:, None]).astype(ml_dtypes.bfloat16).astype(np.float64) / c[:, None] - k
            cost = np.abs(error.sum(1)) / np.abs(k).sum()
            cost = 4.0 * cost + np.sqrt((error**2).sum(1) / (k**2).sum())
            row.append(float(c[np.argmin(cost)]))
        table.append(row)
    return table


def taps_kernel(ctap, cvar, far_tap, near_tap, far_var, near_var, token):
    _, _, lat = where_am_i()
    token[...] = jnp.zeros(token.shape, F32)
    w = iota((256, 128), 0)
    n = iota((256, 128), 1)
    straight = w - n - 64
    wrapped_w = jnp.where(w < 128, 416 + w, w - 160)
    wrapped_n = jnp.where(n < 64, 448 + n, n - 64)
    a = iota((HALF, 128), 0)
    b = iota((HALF, 128), 1)
    table = tap_scales()

    def far_row(p):
        return jnp.where(lat == 0, p, jnp.where(p < HALF, p + HALF, p - 32))

    def near_row(p):
        inner = jnp.where(lat == 0, p + HALF, p)
        adjacent = jnp.where(lat == 0, p - 32, p)
        halo = jnp.where(lat == 0, p + 96, p - 192)
        return jnp.where(p < HALF, inner, jnp.where(p < HALF + 32, adjacent, halo))

    for s in range(SCALES):
        sigma = RAD / 2.0 ** (4 - s)
        chh, chg, cgg = table[s]
        for kind, offset in ((0, straight), (1, wrapped_w - wrapped_n)):
            bell, hat = bell_hat(offset, sigma)
            for k, t in enumerate((hat, bell)):
                high, low = split(t)
                here = slice(256 * s + 128 * k, 256 * s + 128 * k + 128)
                ctap[kind, :256, here] = high
                ctap[kind, 256:512, here] = high
                ctap[kind, 512:, here] = low
            for k, t in enumerate((chh * hat * hat, chg * hat * bell, cgg * bell * bell)):
                here = slice(384 * s + 128 * k, 384 * s + 128 * k + 128)
                t = t.astype(BF16)
                cvar[kind, :256, here] = t
                cvar[kind, 256:, here] = t
        for tap, var, span, place in (
            (far_tap, far_var, FAR_K, far_row),
            (near_tap, near_var, NEAR_K, near_row),
        ):
            for j in range(-(-6 * span // 128)):
                here = slice(128 * j, min(128 * j + 128, 6 * span))
                size = here.stop - here.start
                lane = 128 * j + b
                copy = (lane >= 2 * span).astype(jnp.int32) + (lane >= 4 * span).astype(jnp.int32)
                p = lane - 2 * span * copy
                second = p >= span
                bell, hat = bell_hat(place(jnp.where(second, p - span, p)) - place(a), sigma)
                high, low = split(jnp.where(second, hat, bell))
                t = jnp.where(copy == 1, low.astype(F32), high.astype(F32)).astype(BF16)
                tap[s, :, here] = t[:, :size]
                p = jnp.where(lane >= 3 * span, lane - 3 * span, lane)
                which = (p >= span).astype(jnp.int32) + (p >= 2 * span).astype(jnp.int32)
                bell, hat = bell_hat(place(p - span * which) - place(a), sigma)
                t = jnp.where(which == 1, (2.0 * chg) * hat * bell, chh * hat * hat)
                t = jnp.where(which == 0, cgg * bell * bell, t).astype(BF16)
                var[s, :, here] = t[:, :size]


def mm(a, b):
    return jnp.dot(a, b, preferred_element_type=F32)


def column_filters(size, fields, ctap, cvar, wave, vari, x, xw):
    for j in range(6):
        for f in range(2):
            high, low = split(fields(f, j))
            if j < 4:
                places = [(x, 3 * f + b, j - b) for b in range(3) if j - b in (0, 1)]
            else:
                places = [(xw, f, j - 4)]
            for ref, b, side in places:
                rows = slice(size * b, size * b + size)
                ref[rows, 128 * side : 128 * side + 128] = high
                ref[rows, 256 + 128 * side : 384 + 128 * side] = low
                ref[rows, 512 + 128 * side : 640 + 128 * side] = high
    for f in range(2):
        y = mm(x[3 * size * f : 3 * size * (f + 1), :], ctap[0])
        for s in range(SCALES):
            for k in range(2):
                for b in range(3):
                    wave[s, 2 * f + k, :, 128 * b : 128 * b + 128] = y[
                        size * b : size * b + size, 256 * s + 128 * k : 256 * s + 128 * k + 128
                    ]
    z = mm(x[3 * size :, :512], cvar[0])
    for s in range(SCALES):
        for k in range(3):
            for b in range(3):
                vari[s, k, :, 128 * b : 128 * b + 128] = z[
                    size * b : size * b + size, 384 * s + 128 * k : 384 * s + 128 * k + 128
                ]
    y = mm(xw[...], ctap[1])
    z = mm(xw[size:, :512], cvar[1])
    for s in range(SCALES):
        for k in range(2):
            here = slice(256 * s + 128 * k, 256 * s + 128 * k + 128)
            wave[s, k, :, 384:] = y[:size, here]
            wave[s, 2 + k, :, 384:] = y[size:, here]
        for k in range(3):
            vari[s, k, :, 384:] = z[:, 384 * s + 128 * k : 384 * s + 128 * k + 128]


def near_columns_kernel(total, wrap, ctap, cvar, wave, vari, token, x, xw):
    token[...] = jnp.zeros(token.shape, F32)

    def fields(f, j):
        if j < 4:
            return total[f, :, 128 * j : 128 * j + 128]
        return wrap[f, :, 128 * (j - 4) : 128 * (j - 3)]

    column_filters(HALF, fields, ctap, cvar, wave, vari, x, xw)


def far_columns_kernel(total, outer, inner, lat_rows, ctap, cvar, wave, vari, x, xw):
    _, core, _ = where_am_i()
    wrap = [seam(total[f], outer[f], unpack(inner[f]), core) for f in range(2)]

    def fields(f, j):
        if j < 4:
            mine = total[f, :, 128 * j : 128 * j + 128]
        else:
            mine = wrap[f][:, 128 * (j - 4) : 128 * (j - 3)]
        return jnp.concatenate([mine, lat_rows[f, :, 128 * j : 128 * j + 128]], axis=0)

    column_filters(HALF + RAD, fields, ctap, cvar, wave, vari, x, xw)


def final_kernel(
    near_wave, near_vari, far_wave, far_vari, sums, last,
    far_tap, near_tap, far_var, near_var, out, rate, fw, fv, nw, nv,
):
    _, core, lat = where_am_i()
    whole = sums[...] + last[...]
    own = whole[0:1] / whole[1:2]
    other = whole[2:3] / whole[3:4]
    table = tap_scales()

    def column(row):
        return jnp.transpose(jnp.broadcast_to(row, (128, 128)))

    lo, hi = own[:, :128], own[:, 128:]
    rate[0] = column(jnp.where(lat == 0, lo, hi))
    rate[1] = column(jnp.where(lat == 0, hi, lo))
    halo = column(jnp.where(lat == 0, other[:, :128], other[:, 128:]))
    rate[2, :RAD] = jnp.where(lat == 0, halo[:RAD], halo[96:])
    near_edge = pl.ds(pl.multiple_of(96 * lat, 32), RAD)
    far_edge = pl.ds(pl.multiple_of(96 * (1 - lat), 32), RAD)
    all_rows = slice(0, HALF)
    halo_rows = slice(HALF, HALF + RAD)
    far_parts = ((0, all_rows, 0, all_rows, 0), (1, near_edge, 1, near_edge, HALF))
    near_parts = (
        (1, all_rows, 1, all_rows, 0),
        (0, far_edge, 0, far_edge, HALF),
        (0, halo_rows, 2, slice(0, RAD), HALF + RAD),
    )
    waves = (far_wave, near_wave)
    varis = (far_vari, near_vari)

    def prepare(s):
        factor = [1.0 / (table[s][0] * table[s][2]), 1.0 / table[s][1] ** 2]
        factor.append(factor[0])
        slot = s
        for parts, span, w, v in ((far_parts, FAR_K, fw, fv), (near_parts, NEAR_K, nw, nv)):
            for source, rows, which, rrows, at in parts:
                size = HALF if at == 0 else RAD
                r = rate[which, rrows, :]
                for j in range(4):
                    cols = slice(128 * j, 128 * j + 128)
                    for k in range(2):
                        t = waves[source][s, k, rows, cols] - r * waves[source][s, 2 + k, rows, cols]
                        high, low = split(t)
                        for copy, t in ((0, high), (1, high), (2, low)):
                            first = span * (2 * copy + k) + at
                            w[slot, first : first + size, cols] = t
                    for k in range(3):
                        t = varis[source][s, k, rows, cols] * (r * factor[k])
                        for copy, t in enumerate(split(t)):
                            first = span * (3 * copy + k) + at
                            v[slot, first : first + size, cols] = t

    def multiply(s):
        slot = s
        for w, v, tap, var, start in (
            (fw, fv, far_tap, far_var, HALF * lat),
            (nw, nv, near_tap, near_var, HALF * (1 - lat)),
        ):
            wavelet = mm(tap[s], w[slot])
            variance = mm(var[s], v[slot])
            signal = wavelet * lax.rsqrt(jnp.maximum(variance, 1.0))
            there = pl.ds(pl.multiple_of(start, HALF), HALF)
            out[s, there, :] = pltpu.roll(signal, 64, 1)

    @pl.when(lat >= 0)
    def _():
        for s in range(SCALES):
            prepare(s)

    @pl.when(lat >= 0)
    def _():
        for s in range(SCALES):
            multiply(s)


VMEM = pl.BlockSpec(memory_space=pltpu.VMEM)
ANY = pl.BlockSpec(memory_space=pl.ANY)


def call(kernel, outs, ins, scratch=(), after=(), us=0.01, limit=36):
    count = len(ins)

    def body(*refs):
        kernel(*refs[:count], *refs[count + len(after) :])

    def run(*operands):
        return pl.pallas_call(
            body,
            out_shape=[jax.ShapeDtypeStruct(shape, dtype) for shape, dtype in outs],
            in_specs=list(ins) + [ANY] * len(after),
            out_specs=[VMEM] * len(outs),
            scratch_shapes=list(scratch),
            compiler_params=pltpu.CompilerParams(vmem_limit_bytes=limit * 1024 * 1024),
            cost_estimate=pl.CostEstimate(
                flops=0, bytes_accessed=int(us * 3.6e6), transcendentals=0
            ),
        )(*operands, *after)

    return run


TOKEN = (4, 2 * HALF)
TAPS = [
    ((2, 768, 256 * SCALES), BF16),
    ((2, 512, 384 * SCALES), BF16),
    ((SCALES, HALF, 6 * FAR_K), BF16),
    ((SCALES, HALF, 6 * NEAR_K), BF16),
    ((SCALES, HALF, 6 * FAR_K), BF16),
    ((SCALES, HALF, 6 * NEAR_K), BF16),
]
FINAL_SCRATCH = [pltpu.VMEM((3, HALF, 128), F32)] + [
    pltpu.VMEM((SCALES, 6 * span, TW), BF16) for span in (FAR_K, FAR_K, NEAR_K, NEAR_K)
]


def columns_scratch(rows):
    return [pltpu.VMEM((6 * rows, 768), BF16), pltpu.VMEM((2 * rows, 768), BF16)]


def columns_out(rows):
    return [((SCALES, 4, rows, TW), F32), ((SCALES, 3, rows, TW), F32)]


def per_device(counts_blocks, exposure_blocks, expo_col, expo_count):
    piece = (2, HALF, TW)
    blocks = (4, 2 * HALF, TW)

    def on_lon(value, step):
        return lax.ppermute(value, "lon", [(i, step(i) % LON) for i in range(LON)])

    def two_out(i):
        return i + 2 if i % 2 else i - 2

    def one_out(i):
        return i + 1 if i % 2 else i - 1

    def partner(i):
        return i ^ 1

    inputs = (expo_col, expo_count, counts_blocks, exposure_blocks)
    scalars = [pltpu.SMEM((4,), jnp.int32), pltpu.SMEM((1,), jnp.int32)]
    semaphores = [pltpu.SemaphoreType.DMA((2,)), pltpu.SemaphoreType.DMA((2, 4))]
    b1, sums = call(
        first_kernel,
        [((2, 2 * HALF, TW), F32), ((2, 2 * HALF), F32)],
        [ANY] * 4,
        [pltpu.VMEM((2, 2 * HALF, 128), F32)]
        + scalars
        + [pltpu.VMEM(blocks, jnp.int32), pltpu.VMEM(blocks, F32)]
        + semaphores,
        limit=58,
    )(*inputs)
    sums = sums + on_lon(sums, partner)
    rest = call(
        rest_kernel,
        [(piece, F32)] * 4 + [((2,) + piece, F32)] * 2 + [(TOKEN, F32)],
        [ANY, ANY, VMEM, VMEM],
        [pltpu.VMEM((16, 8, TW), F32)] + scalars + semaphores[:1],
        after=[sums],
        us=1.0,
        limit=24,
    )
    q1n, q1f, q0n, q0f, an, af, rest_token = rest(*inputs)
    an = on_lon(an, partner)
    af = on_lon(af, partner)
    other = lax.ppermute(sums, "lat", [(0, 1), (1, 0)])
    sums = jnp.concatenate([sums, other], axis=0) + rest_token
    b1 = on_lon(b1, two_out)
    steps = [sums]
    (b1_token,) = call(token_kernel, [(TOKEN, F32)], [ANY])(b1)
    sums = sums + on_lon(sums, lambda i: i ^ 16)
    steps.append(sums + b1_token)
    ctap, cvar, far_tap, near_tap, far_var, near_var, taps_token = call(
        taps_kernel, TAPS + [(TOKEN, F32)], [], after=[steps[1]], us=3.0
    )()
    sums = steps[1]
    for flip in (32, 64, 2):
        sums = sums + on_lon(sums, lambda i: i ^ flip)
        if flip == 64:
            sums = sums + taps_token
        steps.append(sums)

    def merge(first, after, *pieces):
        return call(
            functools.partial(merge_kernel, first),
            [(piece, F32), ((2, HALF + 8, TW), F32)],
            [VMEM] * 4,
            after=after,
        )(*pieces)

    def totals(after, *pieces):
        return call(
            total_kernel,
            [(piece, F32), ((2, HALF, 128), F32), ((2, 8, TW), F32)],
            [VMEM] * 3,
            after=after,
        )(*pieces)

    partial_n, sent_n = merge(0, [steps[1]], q1n, q0n, an, b1)
    b2_n = on_lon(sent_n, one_out)
    partial_f, sent_f = merge(HALF, [steps[1]], q1f, q0f, af, b1)
    b2_f = on_lon(sent_f, one_out)
    total_n, outer_n, inner_n = totals([steps[2]], partial_n, b2_n, sent_n)
    inner_n = on_lon(inner_n, partner)
    wrap_n, message = call(
        seam_kernel, [((2, HALF, 256), F32), ((2, RAD, TW + 256), F32)], [VMEM] * 3
    )(total_n, outer_n, inner_n)
    lat_rows = lax.ppermute(message, "lat", [(0, 1), (1, 0)])
    near_wave, near_vari, near_token = call(
        near_columns_kernel,
        columns_out(HALF) + [(TOKEN, F32)],
        [VMEM] * 4,
        columns_scratch(HALF),
        us=4.0,
    )(total_n, wrap_n, ctap, cvar)
    sums = sums + near_token
    sums = sums + on_lon(sums, lambda i: i ^ 4)
    last = on_lon(sums, lambda i: i ^ 8)
    total_f, outer_f, inner_f = totals([steps[3]], partial_f, b2_f, sent_f)
    inner_f = on_lon(inner_f, partner)
    far_wave, far_vari = call(
        far_columns_kernel,
        columns_out(HALF + RAD),
        [VMEM] * 6,
        columns_scratch(HALF + RAD),
        us=5.0,
    )(total_f, outer_f, inner_f, lat_rows, ctap, cvar)
    (out,) = call(
        final_kernel, [((SCALES, 2 * HALF, TW), F32)], [VMEM] * 10, FINAL_SCRATCH
    )(near_wave, near_vari, far_wave, far_vari, sums, last, far_tap, near_tap, far_var, near_var)
    return out


def solution(mesh):
    placed = (P("lon", "lat", None), P("lon", "lat", None), P("lon"), P("lon"))
    return jax.shard_map(
        per_device, mesh=mesh, in_specs=placed, out_specs=P(None, "lat", "lon"), check_vma=False
    )
```
